512 devices in a mesh: grp: 16 (over y, x_hi), emb: 32 (over z, x_lo, core).
Axes of the slice: x: 4 (x_hi: 2, x_lo: 2; x = x_hi * 2 + x_lo), y: 8, z: 8, core: 2. Of those that a mesh axis runs over, the one named last changes fastest.
Arguments:
- pooled: bfloat16 [6144, 256, 192], P(('grp', 'emb')), may hold values from -6 to 6
- upstream: bfloat16 [6144, 256, 192], P(('grp', 'emb')), may hold values from -6 to 6
- ids_now: int32 [6144, 256], P(('grp', 'emb')), may hold values from 0 to 511
- ids_next: int32 [6144, 256], P(('grp', 'emb')), may hold values from 0 to 511
- tables: bfloat16 [256, 512, 192], P('emb'), may hold values from -6 to 6
- w_fm: bfloat16 [256, 128], replicated, may hold values from -0.02734375 to 0.02734375
- w_proj: bfloat16 [128, 192], replicated, may hold values from -0.5 to 0.5
- w_lcb: bfloat16 [256, 256], replicated, may hold values from -0.375 to 0.375
- gain: float32 [192], replicated, may hold values from 0.5 to 1.5
Outputs:
- next_rows: bfloat16 [6144, 256, 192], P(('grp', 'emb'))
- table_grad: float32 [256, 512, 192], P('emb', 'grp')
- grad_fm: float32 [256, 128], replicated
- grad_proj: float32 [128, 192], replicated
- grad_lcb: float32 [256, 256], replicated
- grad_gain: float32 [192], replicated
The draws below stay inside these ranges and needn't reach their ends.
All inputs are finite; a program needn't handle non-finite values.
Results may differ from the reference program's by a relative error of at most 0.017.
Values may be sent and summed in bfloat16 or wider, within the bound.
A program may use at most 64 MiB of HBM per device.

```python
import math
import jax
import jax.numpy as jnp
import numpy as np
from jax import lax

NF = 256
D = 192
K = 128
B_DEV = 12
BATCH = 6144
ROWS = 512
N_GRP = 16
N_EMB = 32


def touch_ends(drawn, key, low, top_value):
    longest = drawn.shape.index(max(drawn.shape))
    spots = []
    for shift in (0, 1):
        where = [jax.random.randint(jax.random.fold_in(key, axis), (), 0, length) for axis, length in enumerate(drawn.shape)]
        where[longest] = (where[longest] + shift) % drawn.shape[longest]
        spots.append(tuple(where))
    return drawn.at[spots[0]].set(low).at[spots[1]].set(top_value)


def level_of(stream_key, shape, pieces, least, high):
    level, own = 1.0, jax.random.fold_in(stream_key, 6)
    for dim, shards_of in pieces:
        draws = jnp.exp(jax.random.uniform(jax.random.fold_in(own, dim), (shards_of,), jnp.float32, least / len(pieces), high / len(pieces)))
        level = level * jnp.repeat(draws, shape[dim] // shards_of).reshape([-1 if axis == dim else 1 for axis in range(len(shape))])
    return level


def rank_table(number_of, lean):
    weights = [(1 << 20) // math.isqrt(grade ** lean) + 1 for grade in range(1, number_of + 1)]
    scale = 1 + sum(weights) // (1 << 30)
    return np.cumsum(np.array([max(1, weight // scale) for weight in weights]))


def ranked_ids(stream_key, extent, count, skew):
    table = rank_table(count, skew)
    lot = jax.random.randint(jax.random.fold_in(stream_key, 1), extent, 0, int(table[count - 1]))
    standing = jnp.searchsorted(jnp.asarray(table, jnp.int32), lot, side="right")
    return jax.random.permutation(jax.random.fold_in(stream_key, 2), count)[standing].astype(jnp.int32)


def normal_values(key, shape, width, bound, cuts=(), dtype=jnp.bfloat16):
    values = jax.random.normal(key, shape, jnp.float32) * width
    if len(cuts) > 0:
        values = level_of(key, shape, cuts, -0.22, 0.18) * values
    return jnp.clip(values, min=-bound, max=bound).astype(dtype)


def setup_inputs(seed: int = 0) -> dict:
    arg_keys = jax.random.split(jax.random.key(seed), 10)
    pooled = normal_values(arg_keys[0], (BATCH, NF, D), 1.0, 6.0, ((0, 512),))
    upstream = normal_values(arg_keys[1], (BATCH, NF, D), 1.0, 6.0, ((0, 512),))
    ids_now = touch_ends(ranked_ids(arg_keys[2], (BATCH, NF), ROWS, 2), jax.random.fold_in(arg_keys[2], 3), 0, ROWS - 1).astype(jnp.int32)
    ids_next = touch_ends(ranked_ids(arg_keys[3], (BATCH, NF), ROWS, 2), jax.random.fold_in(arg_keys[3], 3), 0, ROWS - 1).astype(jnp.int32)
    tables = normal_values(arg_keys[4], (NF, ROWS, D), 1.0, 6.0, ((0, 32),))
    w_fm = normal_values(arg_keys[5], (NF, K), (NF * D) ** -0.5, 0.02734375)
    w_proj = normal_values(arg_keys[6], (K, D), K ** -0.5, 0.5)
    w_lcb = normal_values(arg_keys[7], (NF, NF), NF ** -0.5, 0.375)
    gain = jnp.clip(1.0 + 0.1 * jax.random.normal(arg_keys[8], (D,), jnp.float32), 0.5, 1.5)
    return dict(pooled=pooled, upstream=upstream, ids_now=ids_now, ids_next=ids_next, tables=tables, w_fm=w_fm, w_proj=w_proj, w_lcb=w_lcb, gain=gain)


def product(form, left, right):
    return jnp.einsum(form, left.astype(jnp.float32), right.astype(jnp.float32))

def layer_backward(embeds, cotangent, w_fm, w_proj, w_lcb, gain):
    fm_proj = product('bfc,fj->bcj', embeds, w_fm).astype(jnp.bfloat16)
    fm_rows = product('bfc,bcj->bfj', embeds, fm_proj).astype(jnp.bfloat16)
    projected = product('bfj,jc->bfc', fm_rows, w_proj)
    compressed = product('fi,bfc->bic', w_lcb, embeds)
    summed = embeds.astype(jnp.float32) + projected + compressed
    centre = lax.optimization_barrier(jnp.mean(summed, axis=2, keepdims=True))
    spread = lax.optimization_barrier(jnp.mean((summed - centre) ** 2, axis=2, keepdims=True))
    inverse = lax.rsqrt(spread + 1e-05)
    normed = (summed - centre) * inverse
    upper = cotangent.astype(jnp.float32)
    scaled = upper * gain
    grad_sum = inverse * (scaled - lax.optimization_barrier(jnp.mean(scaled, axis=2, keepdims=True)) - normed * lax.optimization_barrier(jnp.mean(scaled * normed, axis=2, keepdims=True)))
    grad_sum = grad_sum.astype(jnp.bfloat16)
    grad_gain = lax.optimization_barrier(jnp.sum(upper * normed, axis=(0, 1)))
    grad_proj = product('bfj,bfc->jc', fm_rows, grad_sum)
    grad_rows = product('bfc,jc->bfj', grad_sum, w_proj).astype(jnp.bfloat16)
    grad_p = product('bfc,bfj->bcj', embeds, grad_rows).astype(jnp.bfloat16)
    grad_fm = product('bfc,bcj->fj', embeds, grad_p)
    grad_lcb = product('bfc,bic->fi', embeds, grad_sum)
    grad_in = grad_sum.astype(jnp.float32) + product('bfj,bcj->bfc', grad_rows, fm_proj) + product('fj,bcj->bfc', w_fm, grad_p) + product('fi,bic->bfc', w_lcb, grad_sum)
    return (grad_in.astype(jnp.bfloat16), (grad_fm, grad_proj, grad_lcb, grad_gain))

def reference(pooled, upstream, ids_now, ids_next, tables, w_fm, w_proj, w_lcb, gain):
    features = jnp.arange(NF)[None, :]
    next_rows = tables[features, ids_next]
    group_size = B_DEV * N_EMB
    embeds_all = pooled.reshape(N_GRP, group_size, NF, D)
    upper_all = upstream.reshape(N_GRP, group_size, NF, D)
    ids_all = ids_now.reshape(N_GRP, group_size, NF)
    row_index = jnp.arange(ROWS)

    def group_step(carry, inputs):
        embeds, cotangent, ids_group = inputs
        grad_in, partials = layer_backward(embeds, cotangent, w_fm, w_proj, w_lcb, gain)
        indicator = (ids_group.T[:, None, :] == row_index[None, :, None]).astype(jnp.bfloat16)
        part = product('frs,sfc->frc', indicator, grad_in).astype(jnp.bfloat16)
        part = lax.optimization_barrier(part)
        table_total = carry[0] + part.astype(jnp.float32)
        dense = tuple((old + new for old, new in zip(carry[1], partials)))
        return ((table_total, dense), None)
    start = (jnp.zeros((NF, ROWS, D), jnp.float32), (jnp.zeros((NF, K), jnp.float32), jnp.zeros((K, D), jnp.float32), jnp.zeros((NF, NF), jnp.float32), jnp.zeros((D,), jnp.float32)))
    (table_grad, dense), unused = lax.scan(group_step, start, (embeds_all, upper_all, ids_all))
    samples = 1.0 / (B_DEV * N_GRP * N_EMB)
    return (next_rows, table_grad, dense[0] * samples, dense[1] * samples, dense[2] * samples, dense[3] * samples)
```

```python
import functools

import jax
import jax.numpy as jnp
from jax import lax
from jax.experimental import pallas as pl
from jax.experimental.pallas import tpu as pltpu
from jax.sharding import PartitionSpec as P

MESH = pl.DeviceIdType.MESH
BF = jnp.bfloat16
F32 = jnp.float32

NE, NG = 32, 16
B, NF, D, K = 12, 256, 192, 128
FL, ROWS = 8, 512
RG = ROWS // NG
J = B // 2
QUADS = 3
QR = 48
CH = QUADS * QR
DT = NE // 8
KK = DT * 128
FP = 4
PR = 3 * RG
NC = NE // 2
HALF = 512
W1 = 8


def nn(a, b):
    return lax.dot_general(a, b, (((1,), (0,)), ((), ())), preferred_element_type=F32)


def nt(a, b):
    return lax.dot_general(a, b, (((1,), (1,)), ((), ())), preferred_element_type=F32)


def iota(shape, axis):
    return lax.broadcasted_iota(jnp.int32, shape, axis)


def loop(lo, hi, body):
    lax.fori_loop(lo, hi, lambda i, c: (body(i), c)[1], 0)


def kernel(
    x_hbm, u_hbm, now_ref, next_ref, tab_hbm, wfm_ref, wproj_ref, wlcb_ref, gain_ref,
    out_next, out_table, out_fm, out_proj, out_lcb, out_gain,
    xb, ub, tab, idt, ids_s, ids_r, now_k, next_k, main_f, tail_f,
    send_n, recv_n, send_d, recv_d, part_s, part_r,
    gfm, gproj, glcb, ggain, wfm_t, wlcb_t,
    dn_s, dn_p, dn_g, dn_c, dn_own, dn_c2, dn_row, dn_g2, dn_full,
    lsem, id_ss, id_rs, n_ss, n_rs, d_ss, d_rs, p_ss, p_rs,
    pr_ss, pr_rs, g1_ss, g1_rs, c1_ss, c1_rs, c2_ss, c2_rs, g2_ss, g2_rs, pl_ss, pl_rs,
):
    g = lax.axis_index("grp")
    e = lax.axis_index("emb")
    core = lax.rem(e, 2)
    chip = e // 2
    mate = e + 1 - 2 * core

    loads = [
        pltpu.make_async_copy(src, dst, lsem.at[i])
        for i, (src, dst) in enumerate(((x_hbm, xb), (u_hbm, ub), (tab_hbm, tab)))
    ]
    for copy in loads:
        copy.start()

    barrier = pltpu.get_barrier_semaphore()

    def greet_emb(k):
        pl.semaphore_signal(barrier, inc=1, device_id=(g, lax.rem(e + k, NE)), device_id_type=MESH)

    def greet_grp(k):
        pl.semaphore_signal(barrier, inc=1, device_id=(lax.rem(g + k, NG), e), device_id_type=MESH)

    loop(1, NE, greet_emb)
    loop(1, NG, greet_grp)

    def emb_copy(src, dst, ss, rs, t, s):
        return pltpu.make_async_remote_copy(
            src_ref=src, dst_ref=dst, send_sem=ss, recv_sem=rs, device_id=(g, t), device_id_type=MESH)

    def grp_copy(src, dst, ss, rs, t):
        return pltpu.make_async_remote_copy(
            src_ref=src, dst_ref=dst, send_sem=ss, recv_sem=rs, device_id=(t, e), device_id_type=MESH)

    idt[...] = jnp.zeros(idt.shape, jnp.int32)
    idt[0:B, :] = next_ref[...]
    idt[16:16 + B, :] = now_ref[...]
    flipped = jnp.transpose(idt[...])
    lane = iota((NF, 128), 1)
    first, second = lane < J, (lane >= 64) & (lane < 64 + J)
    pad = jnp.where((lane < 8) | ((lane >= 64) & (lane < 72)), -1, 0)
    for kind, base in ((0, 0), (1, 16)):
        low = pltpu.roll(flipped, (128 - base) % 128, axis=1) if base else flipped
        high = pltpu.roll(flipped, 64 - J - base, axis=1)
        tile = jnp.where(first, low, jnp.where(second, high, pad))
        ids_s[kind] = tile.reshape(NE, 8, 128)

    wfm_t[...] = jnp.transpose(wfm_ref[...].astype(F32)).astype(BF)
    wlcb_t[...] = jnp.transpose(wlcb_ref[...].astype(F32)).astype(BF)
    gfm[...] = jnp.zeros(gfm.shape, F32)
    gproj[...] = jnp.zeros(gproj.shape, F32)
    glcb[...] = jnp.zeros(glcb.shape, F32)
    ggain[...] = jnp.zeros(ggain.shape, F32)
    for kind in range(2):
        ids_r[kind, e] = ids_s[kind, e]

    pl.semaphore_wait(barrier, NE - 1 + NG - 1)

    def ids_copy(kind, t, s):
        return emb_copy(ids_s.at[kind, t], ids_r.at[kind, s], id_ss.at[kind, t], id_rs.at[kind, s], t, s)

    for kind in range(2):
        loop(1, NE, lambda k: ids_copy(kind, lax.rem(e + k, NE), e).start())

    def n_copy(t, s):
        return emb_copy(send_n.at[t], recv_n.at[s], n_ss.at[t], n_rs.at[s], t, s)

    def d_copy(t, s):
        return emb_copy(send_d.at[t], recv_d.at[s], d_ss.at[t], d_rs.at[s], t, s)

    for copy in loads[:2]:
        copy.wait()

    wfm, wproj, wlcb = wfm_ref[...], wproj_ref[...], wlcb_ref[...]
    gain = gain_ref[...]

    def sample(b):
        x = xb[b]
        xf = x.astype(F32)
        p_t = nn(wfm_t[...], x).astype(BF)
        rows = nt(x, p_t).astype(BF)
        rows_t = nt(p_t, x).astype(BF)
        s = xf + nn(rows, wproj) + nn(wlcb_t[...], x)
        c = s - jnp.sum(s, axis=1, keepdims=True) * (1.0 / D)
        r = lax.rsqrt(jnp.sum(c * c, axis=1, keepdims=True) * (1.0 / D) + 1e-05)
        z = c * r
        up = ub[b].astype(F32)
        ug = up * gain
        m1 = jnp.sum(ug, axis=1, keepdims=True) * (1.0 / D)
        m2 = jnp.sum(ug * z, axis=1, keepdims=True) * (1.0 / D)
        ds = (r * (ug - m1 - z * m2)).astype(BF)
        ggain[...] += jnp.sum((up * z).reshape(NF // 8, 8, D), axis=0)
        dg = nt(ds, wproj).astype(BF)
        dg_t = nt(wproj, ds).astype(BF)
        dp_t = nn(dg_t, x).astype(BF)
        dx = ds.astype(F32) + nn(dg, p_t) + nn(wfm, dp_t) + nn(wlcb, ds)
        gfm[...] += nt(x, dp_t)
        gproj[...] += nn(rows_t, ds)
        glcb[...] += nt(x, ds)
        return dx

    def quad(q):
        mains, tails = [], []
        for i in range(2):
            pair = [sample(2 * q + i), sample(2 * q + i + J)]
            mains += [dx[:, :128].reshape(NE, 8, 128) for dx in pair]
            tails.append(jnp.concatenate([dx[:, 128:] for dx in pair], axis=1).reshape(NE, 8, 128))
        at = pl.multiple_of(q * QR, 16)
        send_d[:, pl.ds(at, 32), :] = jnp.concatenate(mains, axis=1).astype(BF)
        send_d[:, pl.ds(pl.multiple_of(at + 32, 16), 16), :] = jnp.concatenate(tails, axis=1).astype(BF)

    def lookup():
        loop(1, NE, lambda k: ids_copy(0, e, lax.rem(e + NE - k, NE)).wait_recv())
        for dt in range(DT):
            tile = ids_r[0, dt * 8]
            for d8 in range(1, 8):
                tile = tile + pltpu.roll(ids_r[0, dt * 8 + d8], d8 * 8, axis=1)
            next_k[dt * 8:dt * 8 + 8, :] = tile
        next_k[DT * 8:, :] = jnp.zeros((128 - DT * 8, 128), jnp.int32)
        columns = jnp.transpose(next_k[...])
        row = iota((128, ROWS), 1)
        loads[2].wait()
        for f in range(FL):
            hot = jnp.concatenate(
                [(columns[:, dt * 8 + f:dt * 8 + f + 1] == row).astype(F32).astype(BF) for dt in range(DT)], axis=0)
            got = nn(hot, tab[f])
            for dt in range(DT):
                halves = [got[dt * 128 + 64 * p:dt * 128 + 64 * p + 64] for p in range(2)]
                for p in range(2):
                    main_f[pl.ds(dt * 1024 + 8 * p + f, 64, stride=16), :] = halves[p][:, :128]
                tail_f[pl.ds(dt * 512 + f, 64, stride=8), :] = jnp.concatenate([h[:, 128:] for h in halves], axis=1)

        def pack(d):
            for q in range(QUADS):
                m = pl.multiple_of(d * 128 + q * 32, 32)
                t = pl.multiple_of(d * 64 + q * 16, 16)
                send_n[d, q * QR:q * QR + 32, :] = main_f[pl.ds(m, 32), :].astype(BF)
                send_n[d, q * QR + 32:q * QR + 48, :] = tail_f[pl.ds(t, 16), :].astype(BF)

        loop(0, NE, pack)
        recv_n[e] = send_n[e]
        loop(1, W1 + 1, lambda k: n_copy(lax.rem(e + k, NE), e).start())

    def step(q):
        quad(q)

        @pl.when(q == 0)
        def _():
            lookup()

    loop(0, QUADS, step)

    loop(1, NE, lambda k: d_copy(lax.rem(e + k, NE), e).start())
    recv_d[e] = send_d[e]

    dn_s[0:256, :] = gfm[...]
    dn_s[256:512, :] = glcb[:, :128]
    dn_s[512:768, :] = glcb[:, 128:]
    dn_s[768:896, :] = gproj[:, :128]
    tail = gproj[:, 128:]
    dn_s[896:960, :] = jnp.concatenate([tail[:64], tail[64:]], axis=1)
    total = jnp.sum(ggain[...], axis=0, keepdims=True)
    dn_s[960:968, :] = jnp.broadcast_to(total[:, :128], (8, 128))
    dn_s[968:976, :] = jnp.concatenate(
        [jnp.broadcast_to(total[:, 128:], (8, 64)), jnp.zeros((8, 64), F32)], axis=1)
    dn_s[976:1024, :] = jnp.zeros((48, 128), F32)
    theirs = pl.multiple_of((1 - core) * HALF, HALF)
    mine = pl.multiple_of(core * HALF, HALF)
    pair1 = emb_copy(dn_s.at[pl.ds(theirs, HALF)], dn_p, pr_ss, pr_rs, mate, e)
    pair1.start()

    loop(1, NE, lambda k: ids_copy(1, e, lax.rem(e + NE - k, NE)).wait_recv())
    for dt in range(DT):
        tile = ids_r[1, dt * 8]
        for d8 in range(1, 8):
            tile = tile + pltpu.roll(ids_r[1, dt * 8 + d8], d8 * 8, axis=1)
        now_k[:, dt * 128:dt * 128 + 128] = tile

    pair1.wait_recv()
    dn_p[...] += dn_s[pl.ds(mine, HALF), :]

    def g1_copy(t, s):
        return grp_copy(dn_p.at[pl.ds(pl.multiple_of(t * 32, 32), 32)], dn_g.at[s], g1_ss.at[t], g1_rs.at[s], t)

    loop(1, NG, lambda k: g1_copy(lax.rem(g + k, NG), g).start())
    dn_g[g] = dn_p[pl.ds(pl.multiple_of(g * 32, 32), 32), :]

    loop(1, NG, lambda k: g1_copy(g, lax.rem(g + NG - k, NG)).wait_recv())
    dn_c[...] = jnp.sum(dn_g[...], axis=0).reshape(NC, 2, 128)

    def c1_copy(t, s):
        return emb_copy(dn_c.at[t], dn_c2.at[s], c1_ss.at[t], c1_rs.at[s], 2 * t + core, s)

    loop(1, NC, lambda k: c1_copy(lax.rem(chip + k, NC), chip).start())
    dn_c2[chip] = dn_c[chip]

    def unpack(d):
        for q in range(QUADS):
            m = pl.multiple_of(d * 128 + q * 32, 32)
            t = pl.multiple_of(d * 64 + q * 16, 16)
            main_f[pl.ds(m, 32), :] = recv_d[d, q * QR:q * QR + 32, :].astype(F32)
            tail_f[pl.ds(t, 16), :] = recv_d[d, q * QR + 32:q * QR + 48, :].astype(F32)
        main_f[pl.ds(pl.multiple_of(d * 128 + 96, 32), 32), :] = jnp.zeros((32, 128), F32)
        tail_f[pl.ds(pl.multiple_of(d * 64 + 48, 16), 16), :] = jnp.zeros((16, 128), F32)

    def arrive(k):
        s = lax.rem(e + NE - k, NE)
        d_copy(e, s).wait_recv()
        unpack(s)

    unpack(e)
    loop(1, NE, arrive)

    loop(W1 + 1, NE, lambda k: n_copy(lax.rem(e + k, NE), e).start())

    def p_copy(i, t, s):
        rows = pl.ds(pl.multiple_of(i * PR, PR), PR)
        return grp_copy(part_s.at[t, rows], part_r.at[s, rows], p_ss.at[i, t], p_rs.at[i, s], t)

    row_t = iota((ROWS, KK), 0)
    for i in range(FP):
        parts = []
        for f in (2 * i, 2 * i + 1):
            pieces = []
            for dt in range(DT):
                tail = tail_f[pl.ds(dt * 512 + f, 64, stride=8), :]
                for p in range(2):
                    main = main_f[pl.ds(dt * 1024 + 8 * p + f, 64, stride=16), :]
                    pieces.append(jnp.concatenate([main, tail[:, 64 * p:64 * p + 64]], axis=1))
            terms = jnp.concatenate(pieces, axis=0).astype(BF)
            hot = (row_t == now_k[f:f + 1, :]).astype(F32).astype(BF)
            parts.append(nn(hot, terms))
        part_s[:, i * PR:i * PR + RG, :] = parts[0][:, :128].reshape(NG, RG, 128).astype(BF)
        part_s[:, i * PR + RG:i * PR + 2 * RG, :] = parts[1][:, :128].reshape(NG, RG, 128).astype(BF)
        part_s[:, i * PR + 2 * RG:i * PR + 3 * RG, :] = jnp.concatenate(
            [part[:, 128:] for part in parts], axis=1).reshape(NG, RG, 128).astype(BF)
        loop(1, NG, lambda k: p_copy(i, lax.rem(g + k, NG), g).start())
    part_r[g] = part_s[g]

    loop(1, NC, lambda k: c1_copy(chip, lax.rem(chip + NC - k, NC)).wait_recv())
    dn_own[...] = jnp.sum(dn_c2[...], axis=0)

    def c2_copy(t, s):
        return emb_copy(dn_own, dn_row.at[s], c2_ss.at[t], c2_rs.at[s], 2 * t + core, s)

    loop(1, NC, lambda k: c2_copy(lax.rem(chip + k, NC), chip).start())
    dn_row[chip] = dn_own[...]
    loop(1, NC, lambda k: c2_copy(chip, lax.rem(chip + NC - k, NC)).wait_recv())

    def g2_copy(t, s):
        return grp_copy(dn_row, dn_g2.at[s], g2_ss.at[t], g2_rs.at[s], t)

    loop(1, NG, lambda k: g2_copy(lax.rem(g + k, NG), g).start())
    dn_g2[g] = dn_row[...]

    def place(k):
        s0 = pl.multiple_of(2 * k, 2)
        at = pl.multiple_of(16 * k, 16)
        for q in range(QUADS):
            mains = [recv_n[s0 + i, q * QR:q * QR + 32, :].astype(F32).reshape(4, 8, 128) for i in range(2)]
            tails = [recv_n[s0 + i, q * QR + 32:q * QR + 48, :].astype(F32).reshape(2, 8, 128) for i in range(2)]
            main = jnp.concatenate(mains, axis=1)
            tail = jnp.concatenate(tails, axis=1)
            for i in range(2):
                for p in range(2):
                    out_next[2 * q + i + J * p, pl.ds(at, 16), :] = jnp.concatenate(
                        [main[2 * i + p], tail[i, :, 64 * p:64 * p + 64]], axis=1).astype(BF)

    loop(1, NE, lambda k: n_copy(e, lax.rem(e + NE - k, NE)).wait_recv())
    loop(0, NE // 2, place)

    loop(1, NG, lambda k: g2_copy(g, lax.rem(g + NG - k, NG)).wait_recv())

    def half(h, value):
        dn_full[pl.ds(pl.multiple_of(h * HALF, HALF), HALF), :] = value

    half(core, dn_g2[...].reshape(HALF, 128))
    pair2 = emb_copy(
        dn_full.at[pl.ds(mine, HALF)], dn_full.at[pl.ds(mine, HALF)], pl_ss, pl_rs, mate, e)
    pair2.start()

    for i in range(FP):
        loop(1, NG, lambda k: p_copy(i, g, lax.rem(g + NG - k, NG)).wait_recv())
        total = part_r[0, i * PR:(i + 1) * PR, :].astype(F32)
        for s in range(1, NG):
            total = total + part_r[s, i * PR:(i + 1) * PR, :].astype(F32)
        tail = total[2 * RG:]
        out_table[2 * i] = jnp.concatenate([total[:RG], tail[:, :64]], axis=1)
        out_table[2 * i + 1] = jnp.concatenate([total[RG:2 * RG], tail[:, 64:]], axis=1)

    pair2.wait_recv()
    factor = 1.0 / (B * NE * NG)
    out_fm[...] = dn_full[0:256, :] * factor
    out_lcb[:, :128] = dn_full[256:512, :] * factor
    out_lcb[:, 128:] = dn_full[512:768, :] * factor
    tail = dn_full[896:960, :] * factor
    out_proj[...] = jnp.concatenate(
        [dn_full[768:896, :] * factor, jnp.concatenate([tail[:, :64], tail[:, 64:]], axis=0)], axis=1)
    out_gain[...] = jnp.concatenate([dn_full[960:961, :], dn_full[968:969, :64]], axis=1) * factor

    pair1.wait_send()
    pair2.wait_send()

    def drain_emb(k):
        t = lax.rem(e + k, NE)
        for kind in range(2):
            ids_copy(kind, t, e).wait_send()
        n_copy(t, e).wait_send()
        d_copy(t, e).wait_send()

    def drain_chip(k):
        t = lax.rem(chip + k, NC)
        c1_copy(t, chip).wait_send()
        c2_copy(t, chip).wait_send()

    def drain_grp(k):
        t = lax.rem(g + k, NG)
        g1_copy(t, g).wait_send()
        g2_copy(t, g).wait_send()
        for i in range(FP):
            p_copy(i, t, g).wait_send()

    loop(1, NE, drain_emb)
    loop(1, NC, drain_chip)
    loop(1, NG, drain_grp)


def local(pooled, upstream, ids_now, ids_next, tables, w_fm, w_proj, w_lcb, gain):
    vmem = pl.BlockSpec(memory_space=pltpu.VMEM)
    anywhere = pl.BlockSpec(memory_space=pl.ANY)
    dma = pltpu.SemaphoreType.DMA
    scratch = [
        pltpu.VMEM((B, NF, D), BF), pltpu.VMEM((B, NF, D), BF), pltpu.VMEM((FL, ROWS, D), BF),
        pltpu.VMEM((128, NF), jnp.int32), pltpu.VMEM((2, NE, 8, 128), jnp.int32),
        pltpu.VMEM((2, NE, 8, 128), jnp.int32), pltpu.VMEM((8, KK), jnp.int32),
        pltpu.VMEM((128, 128), jnp.int32),
        pltpu.VMEM((NE * 128, 128), F32), pltpu.VMEM((NE * 64, 128), F32),
        pltpu.VMEM((NE, CH, 128), BF), pltpu.VMEM((NE, CH, 128), BF),
        pltpu.VMEM((NE, CH, 128), BF), pltpu.VMEM((NE, CH, 128), BF),
        pltpu.VMEM((NG, FP * PR, 128), BF), pltpu.VMEM((NG, FP * PR, 128), BF),
        pltpu.VMEM((NF, K), F32), pltpu.VMEM((K, D), F32), pltpu.VMEM((NF, NF), F32), pltpu.VMEM((8, D), F32),
        pltpu.VMEM((K, NF), BF), pltpu.VMEM((NF, NF), BF),
        pltpu.VMEM((2 * HALF, 128), F32), pltpu.VMEM((HALF, 128), F32), pltpu.VMEM((NG, 32, 128), F32),
        pltpu.VMEM((NC, 2, 128), F32), pltpu.VMEM((2, 128), F32), pltpu.VMEM((NC, 2, 128), F32),
        pltpu.VMEM((NC, 2, 128), F32), pltpu.VMEM((NG, NC, 2, 128), F32), pltpu.VMEM((2 * HALF, 128), F32),
        dma((3,)), dma((2, NE)), dma((2, NE)), dma((NE,)), dma((NE,)), dma((NE,)), dma((NE,)),
        dma((FP, NG)), dma((FP, NG)), dma, dma, dma((NG,)), dma((NG,)), dma((NC,)), dma((NC,)),
        dma((NC,)), dma((NC,)), dma((NG,)), dma((NG,)), dma, dma,
    ]
    outs = pl.pallas_call(
        kernel,
        out_shape=(
            jax.ShapeDtypeStruct((B, NF, D), BF),
            jax.ShapeDtypeStruct((FL, RG, D), F32),
            jax.ShapeDtypeStruct((NF, K), F32),
            jax.ShapeDtypeStruct((K, D), F32),
            jax.ShapeDtypeStruct((NF, NF), F32),
            jax.ShapeDtypeStruct((1, D), F32),
        ),
        in_specs=[anywhere, anywhere, vmem, vmem, anywhere, vmem, vmem, vmem, vmem],
        out_specs=[vmem] * 6,
        scratch_shapes=scratch,
        compiler_params=pltpu.CompilerParams(
            collective_id=0, has_side_effects=True, vmem_limit_bytes=48 << 20),
        name="layer_and_tables",
    )(pooled, upstream, ids_now, ids_next, tables, w_fm, w_proj, w_lcb, gain.reshape(1, D))
    return outs[:5] + (outs[5].reshape(D),)


def solution(mesh):
    return jax.shard_map(
        local,
        mesh=mesh,
        in_specs=(
            P(("grp", "emb"), None, None),
            P(("grp", "emb"), None, None),
            P(("grp", "emb"), None),
            P(("grp", "emb"), None),
            P("emb", None, None),
            P(),
            P(),
            P(),
            P(),
        ),
        out_specs=(P(("grp", "emb"), None, None), P("emb", "grp", None), P(), P(), P(), P()),
        check_vma=False,
    )
```

```python
import functools

import jax
import jax.numpy as jnp
from jax import lax
from jax.experimental import pallas as pl
from jax.experimental.pallas import tpu as pltpu
from jax.sharding import PartitionSpec as P

MESH = pl.DeviceIdType.MESH
BF = jnp.bfloat16
F32 = jnp.float32

NE, NG = 32, 16
B, NF, D, K = 12, 256, 192, 128
FL, ROWS = 8, 512
RG = ROWS // NG
J = B // 2
QUADS = 3
QR = 48
CH = QUADS * QR
DT = NE // 8
KK = DT * 128
FP = 4
NY = NG // 2
PR = 3 * RG
NC = NE // 2
HALF = 512
AHEAD = 0
H1, HOLD = 4, 16


def nn(a, b):
    return lax.dot_general(a, b, (((1,), (0,)), ((), ())), preferred_element_type=F32)


def nt(a, b):
    return lax.dot_general(a, b, (((1,), (1,)), ((), ())), preferred_element_type=F32)


def iota(shape, axis):
    return lax.broadcasted_iota(jnp.int32, shape, axis)


def loop(lo, hi, body):
    lax.fori_loop(lo, hi, lambda i, c: (body(i), c)[1], 0)


def kernel(
    x_hbm, u_hbm, now_hbm, next_hbm, tab_hbm, wfm_hbm, wproj_hbm, wlcb_hbm, gain_hbm,
    recv_n, out_table, dn_full,
    xb, ub, tab, wfm_ref, wproj_t, wlcb_ref, gain_ref,
    next_ref, now_ref, idt, ids_s, ids_r, now_k, next_k, main_f, tail_f,
    send_n, send_d, recv_d, part_s, part_x, part_y, part_r,
    gfm_t, gproj_t, glcb_t, ggain, wfm_t, wproj, gain_c,
    dn_s, dn_p, dn_g, dn_c, dn_own, dn_c2, dn_row, dn_g2,
    lsem, id_ss, id_rs, n_ss, n_rs, d_ss, d_rs, px_ss, px_rs, p_ss, p_rs,
    pr_ss, pr_rs, g1_ss, g1_rs, c1_ss, c1_rs, c2_ss, c2_rs, g2_ss, g2_rs, pl_ss, pl_rs,
):
    g = lax.axis_index("grp")
    e = lax.axis_index("emb")
    core = lax.rem(e, 2)
    chip = e // 2
    mate = e + 1 - 2 * core

    loads = [
        pltpu.make_async_copy(src, dst, lsem.at[i])
        for i, (src, dst) in enumerate((
            (next_hbm, next_ref), (now_hbm, now_ref), (wfm_hbm, wfm_ref),
            (wproj_hbm, wproj_t), (gain_hbm, gain_ref), (x_hbm, xb), (wlcb_hbm, wlcb_ref), (u_hbm, ub),
            (tab_hbm, tab)))
    ]
    for copy in loads:
        copy.start()
    idt[...] = jnp.zeros(idt.shape, jnp.int32)

    barrier = pltpu.get_barrier_semaphore()

    def greet_emb(k):
        pl.semaphore_signal(barrier, inc=1, device_id=(g, lax.rem(e + k, NE)), device_id_type=MESH)

    def greet_grp(k):
        pl.semaphore_signal(barrier, inc=1, device_id=(lax.rem(g + k, NG), e), device_id_type=MESH)

    loop(1, NE, greet_emb)
    loop(1, NG, greet_grp)

    def emb_copy(src, dst, ss, rs, t, s):
        return pltpu.make_async_remote_copy(
            src_ref=src, dst_ref=dst, send_sem=ss, recv_sem=rs, device_id=(g, t), device_id_type=MESH)

    def grp_copy(src, dst, ss, rs, t):
        return pltpu.make_async_remote_copy(
            src_ref=src, dst_ref=dst, send_sem=ss, recv_sem=rs, device_id=(t, e), device_id_type=MESH)

    for copy in loads[:5]:
        copy.wait()
    idt[0:B, :] = next_ref[...]
    idt[16:16 + B, :] = now_ref[...]
    flipped = jnp.transpose(idt[...])
    lane = iota((NF, 128), 1)
    tile = jnp.full((NF, 128), -1, jnp.int32)
    for kind in range(2):
        for p in range(2):
            at = 64 * p + 8 * kind
            moved = flipped if kind + p == 0 else pltpu.roll(flipped, (at - 16 * kind - J * p) % 128, axis=1)
            tile = jnp.where((lane >= at) & (lane < at + J), moved, tile)
    ids_s[...] = tile.reshape(NE, 8, 128)

    wfm_t[...] = jnp.transpose(wfm_ref[...].astype(F32)).astype(BF)
    wproj[...] = jnp.transpose(wproj_t[...].astype(F32)).astype(BF)
    gain_c[...] = jnp.transpose(jnp.broadcast_to(gain_ref[...], (128, D)))
    gfm_t[...] = jnp.zeros(gfm_t.shape, F32)
    gproj_t[...] = jnp.zeros(gproj_t.shape, F32)
    glcb_t[...] = jnp.zeros(glcb_t.shape, F32)
    ggain[...] = jnp.zeros(ggain.shape, F32)
    ids_r[e] = ids_s[e]

    def ids_copy(t, s):
        return emb_copy(ids_s.at[t], ids_r.at[s], id_ss.at[t], id_rs.at[s], t, s)

    def ids_tile(kind, dt):
        lane = lax.rem(iota((8, 128), 1), 64)
        tile = jnp.zeros((8, 128), jnp.int32)
        for d8 in range(8):
            moved = pltpu.roll(ids_r[dt * 8 + d8], (8 * d8 - 8 * kind) % 128, axis=1)
            tile = jnp.where((lane >= 8 * d8) & (lane < 8 * d8 + 8), moved, tile)
        return tile

    def n_copy(t, s):
        return emb_copy(send_n.at[t], recv_n.at[s], n_ss.at[t], n_rs.at[s], t, s)

    def d_copy(q, t, s):
        rows = pl.ds(pl.multiple_of(q * QR, QR), QR)
        return emb_copy(send_d.at[t, rows], recv_d.at[s, rows], d_ss.at[q, t], d_rs.at[q, s], t, s)

    for copy in loads[5:8]:
        copy.wait()

    def sample(b):
        x = xb[b]
        p_t = nt(wfm_t[...], x).astype(BF)
        rows_t = nn(p_t, x).astype(BF)
        s = x.astype(F32) + nn(wproj_t[...], rows_t) + nn(x, wlcb_ref[...])
        c = s - jnp.sum(s, axis=0, keepdims=True) * (1.0 / D)
        r = lax.rsqrt(jnp.sum(c * c, axis=0, keepdims=True) * (1.0 / D) + 1e-05)
        z = c * r
        up = ub[b].astype(F32)
        gain = gain_c[...]
        ug = up * jnp.concatenate([gain, gain], axis=1)
        m1 = jnp.sum(ug, axis=0, keepdims=True) * (1.0 / D)
        m2 = jnp.sum(ug * z, axis=0, keepdims=True) * (1.0 / D)
        ds_t = (r * (ug - m1 - z * m2)).astype(BF)
        uz = up * z
        ggain[...] += uz[:, :128] + uz[:, 128:]
        ds_f = jnp.transpose(ds_t.astype(F32))
        ds = ds_f.astype(BF)
        dg_t = nn(wproj[...], ds_t).astype(BF)
        dg = nt(ds, wproj[...]).astype(BF)
        dp_t = nt(dg_t, x).astype(BF)
        dx = ds_f + nn(wlcb_ref[...], ds) + nn(
            jnp.concatenate([dg, wfm_ref[...]], axis=1), jnp.concatenate([p_t, dp_t], axis=0))
        gfm_t[...] += nn(dp_t, x)
        gproj_t[...] += nt(ds_t, rows_t)
        glcb_t[...] += nn(ds, x)
        return dx

    def quad(q):
        mains, tails = [], []
        for i in range(2):
            pair = [sample(2 * q + i), sample(2 * q + i + J)]
            mains += [dx[:, :128].reshape(NE, 8, 128) for dx in pair]
            tails.append(jnp.concatenate([dx[:, 128:] for dx in pair], axis=1).reshape(NE, 8, 128))
        at = pl.multiple_of(q * QR, 16)
        send_d[:, pl.ds(at, 32), :] = jnp.concatenate(mains, axis=1).astype(BF)
        send_d[:, pl.ds(pl.multiple_of(at + 32, 16), 16), :] = jnp.concatenate(tails, axis=1).astype(BF)

    def lookup():
        loop(1, NE, lambda k: ids_copy(e, lax.rem(e + NE - k, NE)).wait_recv())
        for dt in range(DT):
            next_k[dt * 8:dt * 8 + 8, :] = ids_tile(0, dt)
            now_k[:, dt * 128:dt * 128 + 128] = ids_tile(1, dt)
        next_k[DT * 8:, :] = jnp.zeros((128 - DT * 8, 128), jnp.int32)
        columns = jnp.transpose(next_k[...])
        row = iota((128, ROWS), 1)
        loads[8].wait()
        for f in range(FL):
            hot = jnp.concatenate(
                [(columns[:, dt * 8 + f:dt * 8 + f + 1] == row).astype(F32).astype(BF) for dt in range(DT)], axis=0)
            got = nt(hot, tab[f])
            for dt in range(DT):
                halves = [got[dt * 128 + 64 * p:dt * 128 + 64 * p + 64] for p in range(2)]
                for p in range(2):
                    main_f[pl.ds(dt * 1024 + 8 * p + f, 64, stride=16), :] = halves[p][:, :128]
                tail_f[pl.ds(dt * 512 + f, 64, stride=8), :] = jnp.concatenate([h[:, 128:] for h in halves], axis=1)

        def pack(d):
            for q in range(QUADS):
                m = pl.multiple_of(d * 128 + q * 32, 32)
                t = pl.multiple_of(d * 64 + q * 16, 16)
                send_n[d, q * QR:q * QR + 32, :] = main_f[pl.ds(m, 32), :].astype(BF)
                send_n[d, q * QR + 32:q * QR + 48, :] = tail_f[pl.ds(t, 16), :].astype(BF)

        loop(0, NE, pack)
        recv_n[e] = send_n[e]

    def send_quad(q):
        loop(1, NE, lambda k: d_copy(q, lax.rem(e + k, NE), e).start())

    def enter():
        pl.semaphore_wait(barrier, NE - 1 + NG - 1)
        loop(1, NE, lambda k: ids_copy(lax.rem(e + k, NE), e).start())

    if AHEAD == 0:
        enter()

    def step(q):
        quad(q)

        @pl.when(q == AHEAD - 1)
        def _():
            enter()
            for before in range(AHEAD - 1):
                send_quad(before)

        @pl.when(q >= AHEAD - 1)
        def _():
            send_quad(q)

    loop(0, QUADS, step)
    recv_d[e] = send_d[e]

    for h in range(2):
        dn_s[128 * h:128 * h + 128, :] = gfm_t[:, 128 * h:128 * h + 128]
        dn_s[256 + 256 * h:512 + 256 * h, :] = glcb_t[:, 128 * h:128 * h + 128]
    dn_s[768:960, :] = gproj_t[...]
    total = jnp.sum(jnp.transpose(ggain[...]), axis=0, keepdims=True)
    dn_s[960:968, :] = jnp.broadcast_to(total[:, :128], (8, 128))
    dn_s[968:976, :] = jnp.concatenate(
        [jnp.broadcast_to(total[:, 128:], (8, 64)), jnp.zeros((8, 64), F32)], axis=1)
    dn_s[976:1024, :] = jnp.zeros((48, 128), F32)
    theirs = pl.multiple_of((1 - core) * HALF, HALF)
    mine = pl.multiple_of(core * HALF, HALF)
    pair1 = emb_copy(dn_s.at[pl.ds(theirs, HALF)], dn_p, pr_ss, pr_rs, mate, e)
    pair1.start()

    lookup()

    pair1.wait_recv()
    dn_p[...] += dn_s[pl.ds(mine, HALF), :]

    def g1_copy(t, s):
        return grp_copy(dn_p.at[pl.ds(pl.multiple_of(t * 32, 32), 32)], dn_g.at[s], g1_ss.at[t], g1_rs.at[s], t)

    loop(1, NG, lambda k: g1_copy(lax.rem(g + k, NG), g).start())
    dn_g[g] = dn_p[pl.ds(pl.multiple_of(g * 32, 32), 32), :]

    def unpack(d):
        for q in range(QUADS):
            m = pl.multiple_of(d * 128 + q * 32, 32)
            t = pl.multiple_of(d * 64 + q * 16, 16)
            main_f[pl.ds(m, 32), :] = recv_d[d, q * QR:q * QR + 32, :].astype(F32)
            tail_f[pl.ds(t, 16), :] = recv_d[d, q * QR + 32:q * QR + 48, :].astype(F32)
        main_f[pl.ds(pl.multiple_of(d * 128 + 96, 32), 32), :] = jnp.zeros((32, 128), F32)
        tail_f[pl.ds(pl.multiple_of(d * 64 + 48, 16), 16), :] = jnp.zeros((16, 128), F32)

    def arrive(k):
        s = lax.rem(e + NE - k, NE)
        for q in range(QUADS):
            d_copy(q, e, s).wait_recv()
        unpack(s)

    def arrive_send(k):
        arrive(k)
        n_copy(lax.rem(e + k - HOLD + 1, NE), e).start()

    unpack(e)
    loop(1, H1, arrive)

    loop(1, NG, lambda k: g1_copy(g, lax.rem(g + NG - k, NG)).wait_recv())
    dn_c[...] = jnp.sum(dn_g[...], axis=0).reshape(NC, 2, 128)

    def c1_copy(t, s):
        return emb_copy(dn_c.at[t], dn_c2.at[s], c1_ss.at[t], c1_rs.at[s], 2 * t + core, s)

    loop(1, NC, lambda k: c1_copy(lax.rem(chip + k, NC), chip).start())
    dn_c2[chip] = dn_c[chip]

    loop(H1, HOLD, arrive)

    loop(1, NC, lambda k: c1_copy(chip, lax.rem(chip + NC - k, NC)).wait_recv())
    dn_own[...] = jnp.sum(dn_c2[...], axis=0)

    def c2_copy(t, s):
        return emb_copy(dn_own, dn_row.at[s], c2_ss.at[t], c2_rs.at[s], 2 * t + core, s)

    loop(1, NC, lambda k: c2_copy(lax.rem(chip + k, NC), chip).start())
    dn_row[chip] = dn_own[...]
    loop(HOLD, NE, arrive_send)
    loop(NE - HOLD + 1, NE, lambda k: n_copy(lax.rem(e + k, NE), e).start())

    y, xh = g // 2, lax.rem(g, 2)

    def px_copy(i):
        rows = pl.ds(i * PR, PR)
        return pltpu.make_async_remote_copy(
            src_ref=part_s.at[1 - xh, :, rows], dst_ref=part_x.at[:, rows], send_sem=px_ss.at[i],
            recv_sem=px_rs.at[i], device_id=(2 * y + 1 - xh, e), device_id_type=MESH)

    def p_copy(i, t, s):
        rows = pl.ds(pl.multiple_of(i * PR, PR), PR)
        return grp_copy(part_y.at[t, rows], part_r.at[s, rows], p_ss.at[i, t], p_rs.at[i, s], 2 * t + xh)

    row_t = iota((ROWS, KK), 0)
    for i in range(FP):
        parts = []
        for f in (2 * i, 2 * i + 1):
            pieces = []
            for dt in range(DT):
                tail = tail_f[pl.ds(dt * 512 + f, 64, stride=8), :]
                for p in range(2):
                    main = main_f[pl.ds(dt * 1024 + 8 * p + f, 64, stride=16), :]
                    pieces.append(jnp.concatenate([main, tail[:, 64 * p:64 * p + 64]], axis=1))
            terms = jnp.concatenate(pieces, axis=0).astype(BF)
            hot = (row_t == now_k[f:f + 1, :]).astype(F32).astype(BF)
            parts.append(nn(hot, terms))
        mains = [part[:, :128].reshape(NY, 2, RG, 128) for part in parts]
        tail = jnp.concatenate([part[:, 128:] for part in parts], axis=1).reshape(NY, 2, RG, 128)
        for h in range(2):
            part_s[h, :, i * PR:(i + 1) * PR, :] = jnp.concatenate(
                [mains[0][:, h], mains[1][:, h], tail[:, h]], axis=1).astype(BF)
        px_copy(i).start()

    loop(1, NC, lambda k: c2_copy(chip, lax.rem(chip + NC - k, NC)).wait_recv())

    def g2_copy(t, s):
        return grp_copy(dn_row, dn_g2.at[s], g2_ss.at[t], g2_rs.at[s], t)

    loop(1, NG, lambda k: g2_copy(lax.rem(g + k, NG), g).start())
    dn_g2[g] = dn_row[...]

    for i in range(FP):
        rows = slice(i * PR, (i + 1) * PR)
        px_copy(i).wait_recv()
        part_y[:, rows, :] = (part_s[xh, :, rows, :].astype(F32) + part_x[:, rows, :].astype(F32)).astype(BF)
        loop(1, NY, lambda k: p_copy(i, lax.rem(y + k, NY), y).start())
    part_r[y] = part_y[y]

    loop(1, NG, lambda k: g2_copy(g, lax.rem(g + NG - k, NG)).wait_recv())

    def half(h, value):
        dn_full[pl.ds(pl.multiple_of(h * HALF, HALF), HALF), :] = value

    half(core, dn_g2[...].reshape(HALF, 128))
    pair2 = emb_copy(
        dn_full.at[pl.ds(mine, HALF)], dn_full.at[pl.ds(mine, HALF)], pl_ss, pl_rs, mate, e)
    pair2.start()

    loop(1, NE, lambda k: n_copy(e, lax.rem(e + NE - k, NE)).wait_recv())

    for i in range(FP):
        loop(1, NY, lambda k: p_copy(i, y, lax.rem(y + NY - k, NY)).wait_recv())
        total = part_r[0, i * PR:(i + 1) * PR, :].astype(F32)
        for s in range(1, NY):
            total = total + part_r[s, i * PR:(i + 1) * PR, :].astype(F32)
        tail = total[2 * RG:]
        out_table[2 * i] = jnp.concatenate([total[:RG], tail[:, :64]], axis=1)
        out_table[2 * i + 1] = jnp.concatenate([total[RG:2 * RG], tail[:, 64:]], axis=1)

    pair2.wait_recv()

    pair1.wait_send()
    pair2.wait_send()

    def drain_emb(k):
        t = lax.rem(e + k, NE)
        ids_copy(t, e).wait_send()
        n_copy(t, e).wait_send()
        for q in range(QUADS):
            d_copy(q, t, e).wait_send()

    def drain_chip(k):
        t = lax.rem(chip + k, NC)
        c1_copy(t, chip).wait_send()
        c2_copy(t, chip).wait_send()

    def drain_grp(k):
        t = lax.rem(g + k, NG)
        g1_copy(t, g).wait_send()
        g2_copy(t, g).wait_send()

    loop(1, NE, drain_emb)
    loop(1, NC, drain_chip)
    loop(1, NG, drain_grp)
    for i in range(FP):
        px_copy(i).wait_send()
        loop(1, NY, lambda k: p_copy(i, lax.rem(y + k, NY), y).wait_send())


def finish(recv_n, table, dense, out_next, out_table, out_fm, out_proj, out_lcb, out_gain):
    @pl.when(pl.program_id(0) == 0)
    def _():
        out_table[...] = table[...]
        factor = 1.0 / (B * NE * NG)
        for h in range(2):
            rows = pl.ds(128 * h, 128)
            out_fm[rows, :] = jnp.transpose(dense[128 * h:128 * h + 128, :] * factor)
            for w in range(2):
                out_lcb[rows, 128 * w:128 * w + 128] = jnp.transpose(
                    dense[256 + 256 * h + 128 * w:384 + 256 * h + 128 * w, :] * factor)
        out_proj[...] = dense[768:960, :] * factor
        out_gain[...] = jnp.concatenate([dense[960:961, :], dense[968:969, :64]], axis=1) * factor

    tail = recv_n[:, 32:48, :].astype(F32)
    for i in range(2):
        main = recv_n[:, 16 * i:16 * i + 16, :].astype(F32)
        tails = jnp.transpose(tail[:, 8 * i:8 * i + 8].reshape(NF, 128)).astype(BF)
        for p in range(2):
            out_next[p, i, 0:128, :] = jnp.transpose(main[:, 8 * p:8 * p + 8].reshape(NF, 128)).astype(BF)
            out_next[p, i, 128:192, :] = tails[64 * p:64 * p + 64]


def whole(*shape):
    return pl.BlockSpec(shape, lambda q: (0,) * len(shape))


def local(pooled, upstream, ids_now, ids_next, tables, w_fm, w_proj, w_lcb, gain):
    vmem = pl.BlockSpec(memory_space=pltpu.VMEM)
    anywhere = pl.BlockSpec(memory_space=pltpu.HBM)
    dma = pltpu.SemaphoreType.DMA
    scratch = [
        pltpu.VMEM((B, D, NF), BF), pltpu.VMEM((B, D, NF), BF), pltpu.VMEM((FL, D, ROWS), BF),
        pltpu.VMEM((NF, K), BF), pltpu.VMEM((D, K), BF), pltpu.VMEM((NF, NF), BF), pltpu.VMEM((1, D), F32),
        pltpu.VMEM((B, NF), jnp.int32), pltpu.VMEM((B, NF), jnp.int32), pltpu.VMEM((128, NF), jnp.int32),
        pltpu.VMEM((NE, 8, 128), jnp.int32),
        pltpu.VMEM((NE, 8, 128), jnp.int32), pltpu.VMEM((8, KK), jnp.int32),
        pltpu.VMEM((128, 128), jnp.int32),
        pltpu.VMEM((NE * 128, 128), F32), pltpu.VMEM((NE * 64, 128), F32),
        pltpu.VMEM((NE, CH, 128), BF),
        pltpu.VMEM((NE, CH, 128), BF), pltpu.VMEM((NE, CH, 128), BF),
        pltpu.VMEM((2, NY, FP * PR, 128), BF), pltpu.VMEM((NY, FP * PR, 128), BF),
        pltpu.VMEM((NY, FP * PR, 128), BF), pltpu.VMEM((NY, FP * PR, 128), BF),
        pltpu.VMEM((K, NF), F32), pltpu.VMEM((D, K), F32), pltpu.VMEM((NF, NF), F32), pltpu.VMEM((D, 128), F32),
        pltpu.VMEM((K, NF), BF), pltpu.VMEM((K, D), BF), pltpu.VMEM((D, 128), F32),
        pltpu.VMEM((2 * HALF, 128), F32), pltpu.VMEM((HALF, 128), F32), pltpu.VMEM((NG, 32, 128), F32),
        pltpu.VMEM((NC, 2, 128), F32), pltpu.VMEM((2, 128), F32), pltpu.VMEM((NC, 2, 128), F32),
        pltpu.VMEM((NC, 2, 128), F32), pltpu.VMEM((NG, NC, 2, 128), F32),
        dma((9,)), dma((NE,)), dma((NE,)), dma((NE,)), dma((NE,)), dma((QUADS, NE)), dma((QUADS, NE)),
        dma((FP,)), dma((FP,)), dma((FP, NY)), dma((FP, NY)), dma, dma, dma((NG,)), dma((NG,)), dma((NC,)), dma((NC,)),
        dma((NC,)), dma((NC,)), dma((NG,)), dma((NG,)), dma, dma,
    ]
    held = pl.pallas_call(
        kernel,
        out_shape=(
            jax.ShapeDtypeStruct((NE, CH, 128), BF),
            jax.ShapeDtypeStruct((FL, RG, D), F32),
            jax.ShapeDtypeStruct((2 * HALF, 128), F32),
        ),
        in_specs=[anywhere] * 9,
        out_specs=[vmem] * 3,
        scratch_shapes=scratch,
        compiler_params=pltpu.CompilerParams(
            collective_id=0, has_side_effects=True, vmem_limit_bytes=62 << 20),
        name="layer_and_tables",
    )(
        jnp.swapaxes(pooled, 1, 2), jnp.swapaxes(upstream, 1, 2), ids_now, ids_next,
        jnp.swapaxes(tables, 1, 2), w_fm, w_proj.T, w_lcb, gain.reshape(1, D))
    outs = pl.pallas_call(
        finish,
        out_shape=(
            jax.ShapeDtypeStruct((2, J, D, NF), BF),
            jax.ShapeDtypeStruct((FL, RG, D), F32),
            jax.ShapeDtypeStruct((NF, K), F32),
            jax.ShapeDtypeStruct((D, K), F32),
            jax.ShapeDtypeStruct((NF, NF), F32),
            jax.ShapeDtypeStruct((1, D), F32),
        ),
        grid=(QUADS,),
        in_specs=[pl.BlockSpec((NE, QR, 128), lambda q: (0, q, 0)), whole(FL, RG, D), whole(2 * HALF, 128)],
        out_specs=[
            pl.BlockSpec((2, 2, D, NF), lambda q: (0, q, 0, 0)), whole(FL, RG, D), whole(NF, K), whole(D, K),
            whole(NF, NF), whole(1, D)],
        compiler_params=pltpu.CompilerParams(vmem_limit_bytes=62 << 20),
        name="finish",
    )(*held)
    return (
        jnp.swapaxes(outs[0].reshape(B, D, NF), 1, 2), outs[1], outs[2], outs[3].T, outs[4], outs[5].reshape(D))


def solution(mesh):
    return jax.shard_map(
        local,
        mesh=mesh,
        in_specs=(
            P(("grp", "emb"), None, None),
            P(("grp", "emb"), None, None),
            P(("grp", "emb"), None),
            P(("grp", "emb"), None),
            P("emb", None, None),
            P(),
            P(),
            P(),
            P(),
        ),
        out_specs=(P(("grp", "emb"), None, None), P("emb", "grp", None), P(), P(), P(), P()),
        check_vma=False,
    )
```

```python
import jax
import jax.numpy as jnp
from jax import lax
from jax.experimental import pallas as pl
from jax.experimental.pallas import tpu as pltpu
from jax.sharding import PartitionSpec as P

MESH = pl.DeviceIdType.MESH
BF = jnp.bfloat16
F32 = jnp.float32

NE, NG = 32, 16
B, NF, D, K = 12, 256, 192, 128
FL, ROWS = 8, 512
RG = ROWS // NG
J = B // 2
QUADS = 3
QR = 48
CH = QUADS * QR
DT = NE // 8
KK = DT * 128
FP = 4
NY = NG // 2
YF = 2
PR = 3 * RG
NC = NE // 2
HALF = 512
AHEAD = 0
H1, HOLD = 4, 17


def nn(a, b):
    return lax.dot_general(a, b, (((1,), (0,)), ((), ())), preferred_element_type=F32)


def nt(a, b):
    return lax.dot_general(a, b, (((1,), (1,)), ((), ())), preferred_element_type=F32)


def iota(shape, axis):
    return lax.broadcasted_iota(jnp.int32, shape, axis)


def loop(lo, hi, body):
    lax.fori_loop(lo, hi, lambda i, c: (body(i), c)[1], 0)


def kernel(
    x_hbm, u_hbm, now_hbm, next_hbm, tab_hbm, wfm_hbm, wproj_hbm, wlcb_hbm, gain_hbm,
    recv_n, out_table, dn_full,
    xb, ub, tab, wfm_ref, wproj_t, wlcb_ref, gain_ref,
    next_ref, now_ref, idt, ids_s, ids_r, now_k, next_k, main_f, tail_f,
    send_n, send_d, recv_d, part_s, part_x, part_y, part_r, part_z, part_t, part_w, part_v,
    gfm_t, gproj_t, glcb_t, ggain, wfm_t, wproj, gain_c,
    dn_s, dn_p, dn_g, dn_c, dn_own, dn_c2, dn_row, dn_g2,
    lsem, id_ss, id_rs, n_ss, n_rs, d_ss, d_rs, px_ss, px_rs, p_ss, p_rs, z_ss, z_rs, w_ss, w_rs,
    pr_ss, pr_rs, g1_ss, g1_rs, c1_ss, c1_rs, c2_ss, c2_rs, g2_ss, g2_rs, pl_ss, pl_rs,
):
    g = lax.axis_index("grp")
    e = lax.axis_index("emb")
    core = lax.rem(e, 2)
    chip = e // 2
    mate = e + 1 - 2 * core

    loads = [
        pltpu.make_async_copy(src, dst, lsem.at[i])
        for i, (src, dst) in enumerate((
            (next_hbm, next_ref), (now_hbm, now_ref), (wfm_hbm, wfm_ref),
            (wproj_hbm, wproj_t), (gain_hbm, gain_ref), (x_hbm, xb), (wlcb_hbm, wlcb_ref), (u_hbm, ub),
            (tab_hbm, tab)))
    ]
    for copy in loads:
        copy.start()
    idt[...] = jnp.zeros(idt.shape, jnp.int32)

    barrier = pltpu.get_barrier_semaphore()

    def greet_emb(k):
        pl.semaphore_signal(barrier, inc=1, device_id=(g, lax.rem(e + k, NE)), device_id_type=MESH)

    def greet_grp(k):
        pl.semaphore_signal(barrier, inc=1, device_id=(lax.rem(g + k, NG), e), device_id_type=MESH)

    loop(1, NE, greet_emb)
    loop(1, NG, greet_grp)

    def emb_copy(src, dst, ss, rs, t, s):
        return pltpu.make_async_remote_copy(
            src_ref=src, dst_ref=dst, send_sem=ss, recv_sem=rs, device_id=(g, t), device_id_type=MESH)

    def grp_copy(src, dst, ss, rs, t):
        return pltpu.make_async_remote_copy(
            src_ref=src, dst_ref=dst, send_sem=ss, recv_sem=rs, device_id=(t, e), device_id_type=MESH)

    for copy in loads[:5]:
        copy.wait()
    idt[0:B, :] = next_ref[...]
    idt[16:16 + B, :] = now_ref[...]
    flipped = jnp.transpose(idt[...])
    lane = iota((NF, 128), 1)
    tile = jnp.full((NF, 128), -1, jnp.int32)
    for kind in range(2):
        for p in range(2):
            at = 64 * p + 8 * kind
            moved = flipped if kind + p == 0 else pltpu.roll(flipped, (at - 16 * kind - J * p) % 128, axis=1)
            tile = jnp.where((lane >= at) & (lane < at + J), moved, tile)
    ids_s[...] = tile.reshape(NE, 8, 128)

    wfm_t[...] = jnp.transpose(wfm_ref[...].astype(F32)).astype(BF)
    wproj[...] = jnp.transpose(wproj_t[...].astype(F32)).astype(BF)
    gain_c[...] = jnp.transpose(jnp.broadcast_to(gain_ref[...], (128, D)))
    gfm_t[...] = jnp.zeros(gfm_t.shape, F32)
    gproj_t[...] = jnp.zeros(gproj_t.shape, F32)
    glcb_t[...] = jnp.zeros(glcb_t.shape, F32)
    ggain[...] = jnp.zeros(ggain.shape, F32)
    ids_r[e] = ids_s[e]

    def ids_copy(t, s):
        return emb_copy(ids_s.at[t], ids_r.at[s], id_ss.at[t], id_rs.at[s], t, s)

    def ids_tile(kind, dt):
        lane = lax.rem(iota((8, 128), 1), 64)
        tile = jnp.zeros((8, 128), jnp.int32)
        for d8 in range(8):
            moved = pltpu.roll(ids_r[dt * 8 + d8], (8 * d8 - 8 * kind) % 128, axis=1)
            tile = jnp.where((lane >= 8 * d8) & (lane < 8 * d8 + 8), moved, tile)
        return tile

    def n_copy(t, s):
        return emb_copy(send_n.at[t], recv_n.at[s], n_ss.at[t], n_rs.at[s], t, s)

    def d_copy(q, t, s):
        rows = pl.ds(pl.multiple_of(q * QR, QR), QR)
        return emb_copy(send_d.at[t, rows], recv_d.at[s, rows], d_ss.at[q, t], d_rs.at[q, s], t, s)

    for copy in loads[5:8]:
        copy.wait()

    def sample(b):
        x = xb[b]
        p_t = nt(wfm_t[...], x).astype(BF)
        rows_t = nn(p_t, x).astype(BF)
        s = x.astype(F32) + nn(wproj_t[...], rows_t) + nn(x, wlcb_ref[...])
        c = s - jnp.sum(s, axis=0, keepdims=True) * (1.0 / D)
        r = lax.rsqrt(jnp.sum(c * c, axis=0, keepdims=True) * (1.0 / D) + 1e-05)
        z = c * r
        up = ub[b].astype(F32)
        gain = gain_c[...]
        ug = up * jnp.concatenate([gain, gain], axis=1)
        m1 = jnp.sum(ug, axis=0, keepdims=True) * (1.0 / D)
        m2 = jnp.sum(ug * z, axis=0, keepdims=True) * (1.0 / D)
        ds_t = (r * (ug - m1 - z * m2)).astype(BF)
        uz = up * z
        ggain[...] += uz[:, :128] + uz[:, 128:]
        ds_f = jnp.transpose(ds_t.astype(F32))
        ds = ds_f.astype(BF)
        dg_t = nn(wproj[...], ds_t).astype(BF)
        dg = nt(ds, wproj[...]).astype(BF)
        dp_t = nt(dg_t, x).astype(BF)
        dx = ds_f + nn(wlcb_ref[...], ds) + nn(
            jnp.concatenate([dg, wfm_ref[...]], axis=1), jnp.concatenate([p_t, dp_t], axis=0))
        gfm_t[...] += nn(dp_t, x)
        gproj_t[...] += nt(ds_t, rows_t)
        glcb_t[...] += nn(ds, x)
        return dx

    def quad(q):
        mains, tails = [], []
        for i in range(2):
            pair = [sample(2 * q + i), sample(2 * q + i + J)]
            mains += [dx[:, :128].reshape(NE, 8, 128) for dx in pair]
            tails.append(jnp.concatenate([dx[:, 128:] for dx in pair], axis=1).reshape(NE, 8, 128))
        at = pl.multiple_of(q * QR, 16)
        send_d[:, pl.ds(at, 32), :] = jnp.concatenate(mains, axis=1).astype(BF)
        send_d[:, pl.ds(pl.multiple_of(at + 32, 16), 16), :] = jnp.concatenate(tails, axis=1).astype(BF)

    def lookup():
        loop(1, NE, lambda k: ids_copy(e, lax.rem(e + NE - k, NE)).wait_recv())
        for dt in range(DT):
            next_k[dt * 8:dt * 8 + 8, :] = ids_tile(0, dt)
            now_k[:, dt * 128:dt * 128 + 128] = ids_tile(1, dt)
        next_k[DT * 8:, :] = jnp.zeros((128 - DT * 8, 128), jnp.int32)
        columns = jnp.transpose(next_k[...])
        row = iota((128, ROWS), 1)
        loads[8].wait()
        for f in range(FL):
            hot = jnp.concatenate(
                [(columns[:, dt * 8 + f:dt * 8 + f + 1] == row).astype(F32).astype(BF) for dt in range(DT)], axis=0)
            got = nt(hot, tab[f])
            for dt in range(DT):
                halves = [got[dt * 128 + 64 * p:dt * 128 + 64 * p + 64] for p in range(2)]
                for p in range(2):
                    main_f[pl.ds(dt * 1024 + 8 * p + f, 64, stride=16), :] = halves[p][:, :128]
                tail_f[pl.ds(dt * 512 + f, 64, stride=8), :] = jnp.concatenate([h[:, 128:] for h in halves], axis=1)

        def pack(d):
            for q in range(QUADS):
                m = pl.multiple_of(d * 128 + q * 32, 32)
                t = pl.multiple_of(d * 64 + q * 16, 16)
                send_n[d, q * QR:q * QR + 32, :] = main_f[pl.ds(m, 32), :].astype(BF)
                send_n[d, q * QR + 32:q * QR + 48, :] = tail_f[pl.ds(t, 16), :].astype(BF)

        loop(0, NE, pack)
        recv_n[e] = send_n[e]

    def send_quad(q):
        loop(1, NE, lambda k: d_copy(q, lax.rem(e + k, NE), e).start())

    def enter():
        pl.semaphore_wait(barrier, NE - 1 + NG - 1)
        loop(1, NE, lambda k: ids_copy(lax.rem(e + k, NE), e).start())

    if AHEAD == 0:
        enter()

    def step(q):
        quad(q)

        @pl.when(q == AHEAD - 1)
        def _():
            enter()
            for before in range(AHEAD - 1):
                send_quad(before)

        @pl.when(q >= AHEAD - 1)
        def _():
            send_quad(q)

    loop(0, QUADS, step)
    recv_d[e] = send_d[e]

    for h in range(2):
        dn_s[128 * h:128 * h + 128, :] = gfm_t[:, 128 * h:128 * h + 128]
        dn_s[256 + 256 * h:512 + 256 * h, :] = glcb_t[:, 128 * h:128 * h + 128]
    dn_s[768:960, :] = gproj_t[...]
    total = jnp.sum(jnp.transpose(ggain[...]), axis=0, keepdims=True)
    dn_s[960:968, :] = jnp.broadcast_to(total[:, :128], (8, 128))
    dn_s[968:976, :] = jnp.concatenate(
        [jnp.broadcast_to(total[:, 128:], (8, 64)), jnp.zeros((8, 64), F32)], axis=1)
    dn_s[976:1024, :] = jnp.zeros((48, 128), F32)
    theirs = pl.multiple_of((1 - core) * HALF, HALF)
    mine = pl.multiple_of(core * HALF, HALF)
    pair1 = emb_copy(dn_s.at[pl.ds(theirs, HALF)], dn_p, pr_ss, pr_rs, mate, e)
    pair1.start()

    lookup()

    pair1.wait_recv()
    dn_p[...] += dn_s[pl.ds(mine, HALF), :]

    def g1_copy(t, s):
        return grp_copy(dn_p.at[pl.ds(pl.multiple_of(t * 32, 32), 32)], dn_g.at[s], g1_ss.at[t], g1_rs.at[s], t)

    loop(1, NG, lambda k: g1_copy(lax.rem(g + k, NG), g).start())
    dn_g[g] = dn_p[pl.ds(pl.multiple_of(g * 32, 32), 32), :]

    def unpack(d):
        for q in range(QUADS):
            m = pl.multiple_of(d * 128 + q * 32, 32)
            t = pl.multiple_of(d * 64 + q * 16, 16)
            main_f[pl.ds(m, 32), :] = recv_d[d, q * QR:q * QR + 32, :].astype(F32)
            tail_f[pl.ds(t, 16), :] = recv_d[d, q * QR + 32:q * QR + 48, :].astype(F32)
        main_f[pl.ds(pl.multiple_of(d * 128 + 96, 32), 32), :] = jnp.zeros((32, 128), F32)
        tail_f[pl.ds(pl.multiple_of(d * 64 + 48, 16), 16), :] = jnp.zeros((16, 128), F32)

    def arrive(k):
        s = lax.rem(e + NE - k, NE)
        for q in range(QUADS):
            d_copy(q, e, s).wait_recv()
        unpack(s)

    zc, xl = e // 4, lax.rem(chip, 2)

    def n_send(i):
        r = lax.rem(i, NC)
        t = lax.rem(zc + r // 2, NE // 4) * 4 + lax.rem(xl + i // NC, 2) * 2 + lax.rem(core + r, 2)
        n_copy(t, e).start()

    def arrive_send(k):
        arrive(k)
        n_send(k - HOLD + 1)

    unpack(e)
    loop(1, H1, arrive)

    loop(1, NG, lambda k: g1_copy(g, lax.rem(g + NG - k, NG)).wait_recv())
    dn_c[...] = jnp.sum(dn_g[...], axis=0).reshape(NC, 2, 128)

    def c1_copy(t, s):
        return emb_copy(dn_c.at[t], dn_c2.at[s], c1_ss.at[t], c1_rs.at[s], 2 * t + core, s)

    loop(1, NC, lambda k: c1_copy(lax.rem(chip + k, NC), chip).start())
    dn_c2[chip] = dn_c[chip]

    loop(H1, HOLD, arrive)

    loop(1, NC, lambda k: c1_copy(chip, lax.rem(chip + NC - k, NC)).wait_recv())
    dn_own[...] = jnp.sum(dn_c2[...], axis=0)

    def c2_copy(t, s):
        return emb_copy(dn_own, dn_row.at[s], c2_ss.at[t], c2_rs.at[s], 2 * t + core, s)

    loop(1, NC, lambda k: c2_copy(lax.rem(chip + k, NC), chip).start())
    dn_row[chip] = dn_own[...]
    loop(HOLD, NE, arrive_send)
    loop(NE - HOLD + 1, NC, n_send)

    y, xh = g // 2, lax.rem(g, 2)

    def px_copy(i):
        rows = pl.ds(i * PR, PR)
        return pltpu.make_async_remote_copy(
            src_ref=part_s.at[1 - xh, :, rows], dst_ref=part_x.at[:, rows], send_sem=px_ss.at[i],
            recv_sem=px_rs.at[i], device_id=(2 * y + 1 - xh, e), device_id_type=MESH)

    def p_copy(i, t, s):
        rows = pl.ds(pl.multiple_of(i * PR, PR), PR)
        return grp_copy(part_y.at[t, rows], part_r.at[s, rows], p_ss.at[i, t], p_rs.at[i, s], 2 * t + xh)

    def z_copy(i, t, s):
        rows = pl.ds(i * PR, PR)
        return grp_copy(
            part_s.at[:, t, rows], part_z.at[s, :, rows], z_ss.at[i, t], z_rs.at[i, s], 2 * t + xh)

    def w_copy(i):
        rows = pl.ds(i * PR, PR)
        return pltpu.make_async_remote_copy(
            src_ref=part_w.at[rows], dst_ref=part_v.at[rows], send_sem=w_ss.at[i], recv_sem=w_rs.at[i],
            device_id=(2 * y + 1 - xh, e), device_id_type=MESH)

    row_t = iota((ROWS, KK), 0)
    for i in range(FP):
        parts = []
        for f in (2 * i, 2 * i + 1):
            pieces = []
            for dt in range(DT):
                tail = tail_f[pl.ds(dt * 512 + f, 64, stride=8), :]
                for p in range(2):
                    main = main_f[pl.ds(dt * 1024 + 8 * p + f, 64, stride=16), :]
                    pieces.append(jnp.concatenate([main, tail[:, 64 * p:64 * p + 64]], axis=1))
            terms = jnp.concatenate(pieces, axis=0).astype(BF)
            hot = (row_t == now_k[f:f + 1, :]).astype(F32).astype(BF)
            parts.append(nn(hot, terms))
        mains = [part[:, :128].reshape(NY, 2, RG, 128) for part in parts]
        tail = jnp.concatenate([part[:, 128:] for part in parts], axis=1).reshape(NY, 2, RG, 128)
        for h in range(2):
            part_s[h, :, i * PR:(i + 1) * PR, :] = jnp.concatenate(
                [mains[0][:, h], mains[1][:, h], tail[:, h]], axis=1).astype(BF)
        if i < YF:
            loop(1, NY, lambda k: z_copy(i, lax.rem(y + k, NY), y).start())
            part_z[y, :, i * PR:(i + 1) * PR, :] = part_s[:, y, i * PR:(i + 1) * PR, :]
        else:
            px_copy(i).start()

    loop(1, NC, lambda k: c2_copy(chip, lax.rem(chip + NC - k, NC)).wait_recv())

    def g2_copy(t, s):
        return grp_copy(dn_row, dn_g2.at[s], g2_ss.at[t], g2_rs.at[s], t)

    loop(1, NG, lambda k: g2_copy(lax.rem(g + k, NG), g).start())
    dn_g2[g] = dn_row[...]

    for i in range(YF, FP):
        rows = slice(i * PR, (i + 1) * PR)
        px_copy(i).wait_recv()
        part_y[:, rows, :] = (part_s[xh, :, rows, :].astype(F32) + part_x[:, rows, :].astype(F32)).astype(BF)
        loop(1, NY, lambda k: p_copy(i, lax.rem(y + k, NY), y).start())
    loop(NC, NE, n_send)
    part_r[y, YF * PR:, :] = part_y[y, YF * PR:, :]

    for i in range(YF):
        rows = slice(i * PR, (i + 1) * PR)
        loop(1, NY, lambda k: z_copy(i, y, lax.rem(y + NY - k, NY)).wait_recv())
        total = part_z[0, :, rows, :].astype(F32)
        for s in range(1, NY):
            total = total + part_z[s, :, rows, :].astype(F32)
        part_t[:, rows, :] = total
        part_w[rows, :] = part_t[1 - xh, rows, :].astype(BF)
        w_copy(i).start()

    loop(1, NG, lambda k: g2_copy(g, lax.rem(g + NG - k, NG)).wait_recv())

    def half(h, value):
        dn_full[pl.ds(pl.multiple_of(h * HALF, HALF), HALF), :] = value

    half(core, dn_g2[...].reshape(HALF, 128))
    pair2 = emb_copy(
        dn_full.at[pl.ds(mine, HALF)], dn_full.at[pl.ds(mine, HALF)], pl_ss, pl_rs, mate, e)
    pair2.start()

    for i in range(FP):
        rows = slice(i * PR, (i + 1) * PR)
        if i < YF:
            w_copy(i).wait_recv()
            total = part_t[xh, rows, :] + part_v[rows, :].astype(F32)
        else:
            loop(1, NY, lambda k: p_copy(i, y, lax.rem(y + NY - k, NY)).wait_recv())
            total = part_r[0, rows, :].astype(F32)
            for s in range(1, NY):
                total = total + part_r[s, rows, :].astype(F32)
        tail = total[2 * RG:]
        out_table[2 * i] = jnp.concatenate([total[:RG], tail[:, :64]], axis=1)
        out_table[2 * i + 1] = jnp.concatenate([total[RG:2 * RG], tail[:, 64:]], axis=1)

    loop(1, NE, lambda k: n_copy(e, lax.rem(e + NE - k, NE)).wait_recv())

    pair2.wait_recv()

    pair1.wait_send()
    pair2.wait_send()

    def drain_emb(k):
        t = lax.rem(e + k, NE)
        ids_copy(t, e).wait_send()
        n_copy(t, e).wait_send()
        for q in range(QUADS):
            d_copy(q, t, e).wait_send()

    def drain_chip(k):
        t = lax.rem(chip + k, NC)
        c1_copy(t, chip).wait_send()
        c2_copy(t, chip).wait_send()

    def drain_grp(k):
        t = lax.rem(g + k, NG)
        g1_copy(t, g).wait_send()
        g2_copy(t, g).wait_send()

    loop(1, NE, drain_emb)
    loop(1, NC, drain_chip)
    loop(1, NG, drain_grp)
    for i in range(FP):
        if i < YF:
            loop(1, NY, lambda k: z_copy(i, lax.rem(y + k, NY), y).wait_send())
            w_copy(i).wait_send()
        else:
            px_copy(i).wait_send()
            loop(1, NY, lambda k: p_copy(i, lax.rem(y + k, NY), y).wait_send())


def finish(recv_n, table, dense, out_next, out_table, out_fm, out_proj, out_lcb, out_gain):
    @pl.when(pl.program_id(0) == 0)
    def _():
        out_table[...] = table[...]
        factor = 1.0 / (B * NE * NG)
        for h in range(2):
            rows = pl.ds(128 * h, 128)
            out_fm[rows, :] = jnp.transpose(dense[128 * h:128 * h + 128, :] * factor)
            for w in range(2):
                out_lcb[rows, 128 * w:128 * w + 128] = jnp.transpose(
                    dense[256 + 256 * h + 128 * w:384 + 256 * h + 128 * w, :] * factor)
        out_proj[...] = dense[768:960, :] * factor
        out_gain[...] = jnp.concatenate([dense[960:961, :], dense[968:969, :64]], axis=1) * factor

    tail = recv_n[:, 32:48, :].astype(F32)
    for i in range(2):
        main = recv_n[:, 16 * i:16 * i + 16, :].astype(F32)
        tails = jnp.transpose(tail[:, 8 * i:8 * i + 8].reshape(NF, 128)).astype(BF)
        for p in range(2):
            out_next[p, i, 0:128, :] = jnp.transpose(main[:, 8 * p:8 * p + 8].reshape(NF, 128)).astype(BF)
            out_next[p, i, 128:192, :] = tails[64 * p:64 * p + 64]


def whole(*shape):
    return pl.BlockSpec(shape, lambda q: (0,) * len(shape))


def local(pooled, upstream, ids_now, ids_next, tables, w_fm, w_proj, w_lcb, gain):
    vmem = pl.BlockSpec(memory_space=pltpu.VMEM)
    anywhere = pl.BlockSpec(memory_space=pltpu.HBM)
    dma = pltpu.SemaphoreType.DMA
    scratch = [
        pltpu.VMEM((B, D, NF), BF), pltpu.VMEM((B, D, NF), BF), pltpu.VMEM((FL, D, ROWS), BF),
        pltpu.VMEM((NF, K), BF), pltpu.VMEM((D, K), BF), pltpu.VMEM((NF, NF), BF), pltpu.VMEM((1, D), F32),
        pltpu.VMEM((B, NF), jnp.int32), pltpu.VMEM((B, NF), jnp.int32), pltpu.VMEM((128, NF), jnp.int32),
        pltpu.VMEM((NE, 8, 128), jnp.int32),
        pltpu.VMEM((NE, 8, 128), jnp.int32), pltpu.VMEM((8, KK), jnp.int32),
        pltpu.VMEM((128, 128), jnp.int32),
        pltpu.VMEM((NE * 128, 128), F32), pltpu.VMEM((NE * 64, 128), F32),
        pltpu.VMEM((NE, CH, 128), BF),
        pltpu.VMEM((NE, CH, 128), BF), pltpu.VMEM((NE, CH, 128), BF),
        pltpu.VMEM((2, NY, FP * PR, 128), BF), pltpu.VMEM((NY, FP * PR, 128), BF),
        pltpu.VMEM((NY, FP * PR, 128), BF), pltpu.VMEM((NY, FP * PR, 128), BF),
        pltpu.VMEM((NY, 2, YF * PR, 128), BF), pltpu.VMEM((2, YF * PR, 128), F32),
        pltpu.VMEM((YF * PR, 128), BF), pltpu.VMEM((YF * PR, 128), BF),
        pltpu.VMEM((K, NF), F32), pltpu.VMEM((D, K), F32), pltpu.VMEM((NF, NF), F32), pltpu.VMEM((D, 128), F32),
        pltpu.VMEM((K, NF), BF), pltpu.VMEM((K, D), BF), pltpu.VMEM((D, 128), F32),
        pltpu.VMEM((2 * HALF, 128), F32), pltpu.VMEM((HALF, 128), F32), pltpu.VMEM((NG, 32, 128), F32),
        pltpu.VMEM((NC, 2, 128), F32), pltpu.VMEM((2, 128), F32), pltpu.VMEM((NC, 2, 128), F32),
        pltpu.VMEM((NC, 2, 128), F32), pltpu.VMEM((NG, NC, 2, 128), F32),
        dma((9,)), dma((NE,)), dma((NE,)), dma((NE,)), dma((NE,)), dma((QUADS, NE)), dma((QUADS, NE)),
        dma((FP,)), dma((FP,)), dma((FP, NY)), dma((FP, NY)),
        dma((YF, NY)), dma((YF, NY)), dma((YF,)), dma((YF,)), dma, dma, dma((NG,)), dma((NG,)), dma((NC,)), dma((NC,)),
        dma((NC,)), dma((NC,)), dma((NG,)), dma((NG,)), dma, dma,
    ]
    held = pl.pallas_call(
        kernel,
        out_shape=(
            jax.ShapeDtypeStruct((NE, CH, 128), BF),
            jax.ShapeDtypeStruct((FL, RG, D), F32),
            jax.ShapeDtypeStruct((2 * HALF, 128), F32),
        ),
        in_specs=[anywhere] * 9,
        out_specs=[vmem] * 3,
        scratch_shapes=scratch,
        compiler_params=pltpu.CompilerParams(
            collective_id=0, has_side_effects=True, vmem_limit_bytes=62 << 20),
        name="layer_and_tables",
    )(
        jnp.swapaxes(pooled, 1, 2), jnp.swapaxes(upstream, 1, 2), ids_now, ids_next,
        jnp.swapaxes(tables, 1, 2), w_fm, w_proj.T, w_lcb, gain.reshape(1, D))
    outs = pl.pallas_call(
        finish,
        out_shape=(
            jax.ShapeDtypeStruct((2, J, D, NF), BF),
            jax.ShapeDtypeStruct((FL, RG, D), F32),
            jax.ShapeDtypeStruct((NF, K), F32),
            jax.ShapeDtypeStruct((D, K), F32),
            jax.ShapeDtypeStruct((NF, NF), F32),
            jax.ShapeDtypeStruct((1, D), F32),
        ),
        grid=(QUADS,),
        in_specs=[pl.BlockSpec((NE, QR, 128), lambda q: (0, q, 0)), whole(FL, RG, D), whole(2 * HALF, 128)],
        out_specs=[
            pl.BlockSpec((2, 2, D, NF), lambda q: (0, q, 0, 0)), whole(FL, RG, D), whole(NF, K), whole(D, K),
            whole(NF, NF), whole(1, D)],
        compiler_params=pltpu.CompilerParams(vmem_limit_bytes=62 << 20),
        name="finish",
    )(*held)
    return (
        jnp.swapaxes(outs[0].reshape(B, D, NF), 1, 2), outs[1], outs[2], outs[3].T, outs[4], outs[5].reshape(D))


def solution(mesh):
    return jax.shard_map(
        local,
        mesh=mesh,
        in_specs=(
            P(("grp", "emb"), None, None),
            P(("grp", "emb"), None, None),
            P(("grp", "emb"), None),
            P(("grp", "emb"), None),
            P("emb", None, None),
            P(),
            P(),
            P(),
            P(),
        ),
        out_specs=(P(("grp", "emb"), None, None), P("emb", "grp", None), P(), P(), P(), P()),
        check_vma=False,
    )
```

```python
import jax
import jax.numpy as jnp
from jax import lax
from jax.experimental import pallas as pl
from jax.experimental.pallas import tpu as pltpu
from jax.sharding import PartitionSpec as P

MESH = pl.DeviceIdType.MESH
BF = jnp.bfloat16
F32 = jnp.float32

NE, NG = 32, 16
B, NF, D, K = 12, 256, 192, 128
FL, ROWS = 8, 512
RG = ROWS // NG
J = B // 2
QUADS = 3
QR = 48
CH = QUADS * QR
DT = NE // 8
KK = DT * 128
FP = 4
NY = NG // 2
YF = 2
PR = 3 * RG
NC = NE // 2
HALF = 512
AHEAD = 0
H1, HOLD = 4, 17


def nn(a, b):
    return lax.dot_general(a, b, (((1,), (0,)), ((), ())), preferred_element_type=F32)


def nt(a, b):
    return lax.dot_general(a, b, (((1,), (1,)), ((), ())), preferred_element_type=F32)


def iota(shape, axis):
    return lax.broadcasted_iota(jnp.int32, shape, axis)


def loop(lo, hi, body):
    lax.fori_loop(lo, hi, lambda i, c: (body(i), c)[1], 0)


def kernel(
    x_hbm, u_hbm, now_hbm, next_hbm, tab_hbm, wfm_hbm, wproj_hbm, wlcb_hbm, gain_hbm,
    recv_n, out_table, dn_full,
    xb, ub, tab, wfm_ref, wproj_t, wlcb_ref, gain_ref,
    next_ref, now_ref, idt, ids_s, ids_r, now_k, next_k, main_f, tail_f,
    send_n, send_d, recv_d, part_s, part_x, part_y, part_r, part_z, part_t, part_w, part_v,
    gfm_t, gproj_t, glcb_t, ggain, wfm_t, wproj, gain_c,
    dn_s, dn_p, dn_g, dn_c, dn_own, dn_c2, dn_row, dn_row16, dn_g2,
    lsem, id_ss, id_rs, n_ss, n_rs, d_ss, d_rs, px_ss, px_rs, p_ss, p_rs, z_ss, z_rs, w_ss, w_rs,
    pr_ss, pr_rs, g1_ss, g1_rs, c1_ss, c1_rs, c2_ss, c2_rs, g2_ss, g2_rs, pl_ss, pl_rs,
):
    g = lax.axis_index("grp")
    e = lax.axis_index("emb")
    core = lax.rem(e, 2)
    chip = e // 2
    mate = e + 1 - 2 * core

    loads = [
        pltpu.make_async_copy(src, dst, lsem.at[i])
        for i, (src, dst) in enumerate((
            (next_hbm, next_ref), (now_hbm, now_ref), (wfm_hbm, wfm_ref),
            (wproj_hbm, wproj_t), (gain_hbm, gain_ref), (x_hbm, xb), (wlcb_hbm, wlcb_ref), (u_hbm, ub),
            (tab_hbm, tab)))
    ]
    for copy in loads:
        copy.start()
    idt[...] = jnp.zeros(idt.shape, jnp.int32)

    barrier = pltpu.get_barrier_semaphore()

    def greet_emb(k):
        pl.semaphore_signal(barrier, inc=1, device_id=(g, lax.rem(e + k, NE)), device_id_type=MESH)

    def greet_grp(k):
        pl.semaphore_signal(barrier, inc=1, device_id=(lax.rem(g + k, NG), e), device_id_type=MESH)

    loop(1, NE, greet_emb)
    loop(1, NG, greet_grp)

    def emb_copy(src, dst, ss, rs, t, s):
        return pltpu.make_async_remote_copy(
            src_ref=src, dst_ref=dst, send_sem=ss, recv_sem=rs, device_id=(g, t), device_id_type=MESH)

    def grp_copy(src, dst, ss, rs, t):
        return pltpu.make_async_remote_copy(
            src_ref=src, dst_ref=dst, send_sem=ss, recv_sem=rs, device_id=(t, e), device_id_type=MESH)

    for copy in loads[:5]:
        copy.wait()
    idt[0:B, :] = next_ref[...]
    idt[16:16 + B, :] = now_ref[...]
    flipped = jnp.transpose(idt[...])
    lane = iota((NF, 128), 1)
    tile = jnp.full((NF, 128), -1, jnp.int32)
    for kind in range(2):
        for p in range(2):
            at = 64 * p + 8 * kind
            moved = flipped if kind + p == 0 else pltpu.roll(flipped, (at - 16 * kind - J * p) % 128, axis=1)
            tile = jnp.where((lane >= at) & (lane < at + J), moved, tile)
    ids_s[...] = tile.reshape(NE, 8, 128)

    wfm_t[...] = jnp.transpose(wfm_ref[...].astype(F32)).astype(BF)
    wproj[...] = jnp.transpose(wproj_t[...].astype(F32)).astype(BF)
    gain_c[...] = jnp.transpose(jnp.broadcast_to(gain_ref[...], (128, D)))
    gfm_t[...] = jnp.zeros(gfm_t.shape, F32)
    gproj_t[...] = jnp.zeros(gproj_t.shape, F32)
    glcb_t[...] = jnp.zeros(glcb_t.shape, F32)
    ggain[...] = jnp.zeros(ggain.shape, F32)
    ids_r[e] = ids_s[e]

    def ids_copy(t, s):
        return emb_copy(ids_s.at[t], ids_r.at[s], id_ss.at[t], id_rs.at[s], t, s)

    def ids_tile(kind, dt):
        lane = lax.rem(iota((8, 128), 1), 64)
        tile = jnp.zeros((8, 128), jnp.int32)
        for d8 in range(8):
            moved = pltpu.roll(ids_r[dt * 8 + d8], (8 * d8 - 8 * kind) % 128, axis=1)
            tile = jnp.where((lane >= 8 * d8) & (lane < 8 * d8 + 8), moved, tile)
        return tile

    def n_copy(t, s):
        return emb_copy(send_n.at[t], recv_n.at[s], n_ss.at[t], n_rs.at[s], t, s)

    def d_copy(q, t, s):
        rows = pl.ds(pl.multiple_of(q * QR, QR), QR)
        return emb_copy(send_d.at[t, rows], recv_d.at[s, rows], d_ss.at[q, t], d_rs.at[q, s], t, s)

    for copy in loads[5:8]:
        copy.wait()

    def sample(b):
        x = xb[b]
        p_t = nt(wfm_t[...], x).astype(BF)
        rows_t = nn(p_t, x).astype(BF)
        s = x.astype(F32) + nn(wproj_t[...], rows_t) + nn(x, wlcb_ref[...])
        c = s - jnp.sum(s, axis=0, keepdims=True) * (1.0 / D)
        r = lax.rsqrt(jnp.sum(c * c, axis=0, keepdims=True) * (1.0 / D) + 1e-05)
        z = c * r
        up = ub[b].astype(F32)
        gain = gain_c[...]
        ug = up * jnp.concatenate([gain, gain], axis=1)
        m1 = jnp.sum(ug, axis=0, keepdims=True) * (1.0 / D)
        m2 = jnp.sum(ug * z, axis=0, keepdims=True) * (1.0 / D)
        ds_t = (r * (ug - m1 - z * m2)).astype(BF)
        uz = up * z
        ggain[...] += uz[:, :128] + uz[:, 128:]
        ds_f = jnp.transpose(ds_t.astype(F32))
        ds = ds_f.astype(BF)
        dg_t = nn(wproj[...], ds_t).astype(BF)
        dg = nt(ds, wproj[...]).astype(BF)
        dp_t = nt(dg_t, x).astype(BF)
        dx = ds_f + nn(wlcb_ref[...], ds) + nn(
            jnp.concatenate([dg, wfm_ref[...]], axis=1), jnp.concatenate([p_t, dp_t], axis=0))
        gfm_t[...] += nn(dp_t, x)
        gproj_t[...] += nt(ds_t, rows_t)
        glcb_t[...] += nn(ds, x)
        return dx

    def quad(q):
        mains, tails = [], []
        for i in range(2):
            pair = [sample(2 * q + i), sample(2 * q + i + J)]
            mains += [dx[:, :128].reshape(NE, 8, 128) for dx in pair]
            tails.append(jnp.concatenate([dx[:, 128:] for dx in pair], axis=1).reshape(NE, 8, 128))
        at = pl.multiple_of(q * QR, 16)
        send_d[:, pl.ds(at, 32), :] = jnp.concatenate(mains, axis=1).astype(BF)
        send_d[:, pl.ds(pl.multiple_of(at + 32, 16), 16), :] = jnp.concatenate(tails, axis=1).astype(BF)

    def lookup():
        loop(1, NE, lambda k: ids_copy(e, lax.rem(e + NE - k, NE)).wait_recv())
        for dt in range(DT):
            next_k[dt * 8:dt * 8 + 8, :] = ids_tile(0, dt)
            now_k[:, dt * 128:dt * 128 + 128] = ids_tile(1, dt)
        next_k[DT * 8:, :] = jnp.zeros((128 - DT * 8, 128), jnp.int32)
        columns = jnp.transpose(next_k[...])
        row = iota((128, ROWS), 1)
        loads[8].wait()
        for f in range(FL):
            hot = jnp.concatenate(
                [(columns[:, dt * 8 + f:dt * 8 + f + 1] == row).astype(F32).astype(BF) for dt in range(DT)], axis=0)
            got = nt(hot, tab[f])
            for dt in range(DT):
                halves = [got[dt * 128 + 64 * p:dt * 128 + 64 * p + 64] for p in range(2)]
                for p in range(2):
                    main_f[pl.ds(dt * 1024 + 8 * p + f, 64, stride=16), :] = halves[p][:, :128]
                tail_f[pl.ds(dt * 512 + f, 64, stride=8), :] = jnp.concatenate([h[:, 128:] for h in halves], axis=1)

        def pack(d):
            for q in range(QUADS):
                m = pl.multiple_of(d * 128 + q * 32, 32)
                t = pl.multiple_of(d * 64 + q * 16, 16)
                send_n[d, q * QR:q * QR + 32, :] = main_f[pl.ds(m, 32), :].astype(BF)
                send_n[d, q * QR + 32:q * QR + 48, :] = tail_f[pl.ds(t, 16), :].astype(BF)

        loop(0, NE, pack)
        recv_n[e] = send_n[e]

    def send_quad(q):
        loop(1, NE, lambda k: d_copy(q, lax.rem(e + k, NE), e).start())

    def enter():
        pl.semaphore_wait(barrier, NE - 1 + NG - 1)
        loop(1, NE, lambda k: ids_copy(lax.rem(e + k, NE), e).start())

    if AHEAD == 0:
        enter()

    def step(q):
        quad(q)

        @pl.when(q == AHEAD - 1)
        def _():
            enter()
            for before in range(AHEAD - 1):
                send_quad(before)

        @pl.when(q >= AHEAD - 1)
        def _():
            send_quad(q)

    loop(0, QUADS, step)
    recv_d[e] = send_d[e]

    for h in range(2):
        dn_s[128 * h:128 * h + 128, :] = gfm_t[:, 128 * h:128 * h + 128]
        dn_s[256 + 256 * h:512 + 256 * h, :] = glcb_t[:, 128 * h:128 * h + 128]
    dn_s[768:960, :] = gproj_t[...]
    total = jnp.sum(jnp.transpose(ggain[...]), axis=0, keepdims=True)
    dn_s[960:968, :] = jnp.broadcast_to(total[:, :128], (8, 128))
    dn_s[968:976, :] = jnp.concatenate(
        [jnp.broadcast_to(total[:, 128:], (8, 64)), jnp.zeros((8, 64), F32)], axis=1)
    dn_s[976:1024, :] = jnp.zeros((48, 128), F32)
    theirs = pl.multiple_of((1 - core) * HALF, HALF)
    mine = pl.multiple_of(core * HALF, HALF)
    pair1 = emb_copy(dn_s.at[pl.ds(theirs, HALF)], dn_p, pr_ss, pr_rs, mate, e)
    pair1.start()

    lookup()

    pair1.wait_recv()
    dn_p[...] += dn_s[pl.ds(mine, HALF), :]

    def g1_copy(t, s):
        return grp_copy(dn_p.at[pl.ds(pl.multiple_of(t * 32, 32), 32)], dn_g.at[s], g1_ss.at[t], g1_rs.at[s], t)

    loop(1, NG, lambda k: g1_copy(lax.rem(g + k, NG), g).start())
    dn_g[g] = dn_p[pl.ds(pl.multiple_of(g * 32, 32), 32), :]

    def unpack(d):
        for q in range(QUADS):
            m = pl.multiple_of(d * 128 + q * 32, 32)
            t = pl.multiple_of(d * 64 + q * 16, 16)
            main_f[pl.ds(m, 32), :] = recv_d[d, q * QR:q * QR + 32, :].astype(F32)
            tail_f[pl.ds(t, 16), :] = recv_d[d, q * QR + 32:q * QR + 48, :].astype(F32)
        main_f[pl.ds(pl.multiple_of(d * 128 + 96, 32), 32), :] = jnp.zeros((32, 128), F32)
        tail_f[pl.ds(pl.multiple_of(d * 64 + 48, 16), 16), :] = jnp.zeros((16, 128), F32)

    def arrive(k):
        s = lax.rem(e + NE - k, NE)
        for q in range(QUADS):
            d_copy(q, e, s).wait_recv()
        unpack(s)

    zc, xl = e // 4, lax.rem(chip, 2)

    def n_send(i):
        r = lax.rem(i, NC)
        t = lax.rem(zc + r // 2, NE // 4) * 4 + lax.rem(xl + i // NC, 2) * 2 + lax.rem(core + r, 2)
        n_copy(t, e).start()

    def arrive_send(k):
        arrive(k)
        n_send(k - HOLD + 1)

    unpack(e)
    loop(1, H1, arrive)

    loop(1, NG, lambda k: g1_copy(g, lax.rem(g + NG - k, NG)).wait_recv())
    dn_c[...] = jnp.sum(dn_g[...], axis=0).reshape(NC, 2, 128)

    def c1_copy(t, s):
        return emb_copy(dn_c.at[t], dn_c2.at[s], c1_ss.at[t], c1_rs.at[s], 2 * t + core, s)

    loop(1, NC, lambda k: c1_copy(lax.rem(chip + k, NC), chip).start())
    dn_c2[chip] = dn_c[chip]

    loop(H1, HOLD, arrive)

    loop(1, NC, lambda k: c1_copy(chip, lax.rem(chip + NC - k, NC)).wait_recv())
    dn_own[...] = jnp.sum(dn_c2[...], axis=0)

    def c2_copy(t, s):
        return emb_copy(dn_own, dn_row.at[s], c2_ss.at[t], c2_rs.at[s], 2 * t + core, s)

    loop(1, NC, lambda k: c2_copy(lax.rem(chip + k, NC), chip).start())
    dn_row[chip] = dn_own[...]
    loop(HOLD, NE, arrive_send)
    loop(NE - HOLD + 1, NC, n_send)

    y, xh = g // 2, lax.rem(g, 2)

    def px_copy(i):
        rows = pl.ds(i * PR, PR)
        return pltpu.make_async_remote_copy(
            src_ref=part_s.at[1 - xh, :, rows], dst_ref=part_x.at[:, rows], send_sem=px_ss.at[i],
            recv_sem=px_rs.at[i], device_id=(2 * y + 1 - xh, e), device_id_type=MESH)

    def p_copy(i, t, s):
        rows = pl.ds(pl.multiple_of(i * PR, PR), PR)
        return grp_copy(part_y.at[t, rows], part_r.at[s, rows], p_ss.at[i, t], p_rs.at[i, s], 2 * t + xh)

    def z_copy(i, t, s):
        rows = pl.ds(i * PR, PR)
        return grp_copy(
            part_s.at[:, t, rows], part_z.at[s, :, rows], z_ss.at[i, t], z_rs.at[i, s], 2 * t + xh)

    def w_copy(i):
        rows = pl.ds(i * PR, PR)
        return pltpu.make_async_remote_copy(
            src_ref=part_w.at[rows], dst_ref=part_v.at[rows], send_sem=w_ss.at[i], recv_sem=w_rs.at[i],
            device_id=(2 * y + 1 - xh, e), device_id_type=MESH)

    row_t = iota((ROWS, KK), 0)
    for i in range(FP):
        parts = []
        for f in (2 * i, 2 * i + 1):
            pieces = []
            for dt in range(DT):
                tail = tail_f[pl.ds(dt * 512 + f, 64, stride=8), :]
                for p in range(2):
                    main = main_f[pl.ds(dt * 1024 + 8 * p + f, 64, stride=16), :]
                    pieces.append(jnp.concatenate([main, tail[:, 64 * p:64 * p + 64]], axis=1))
            terms = jnp.concatenate(pieces, axis=0).astype(BF)
            hot = (row_t == now_k[f:f + 1, :]).astype(F32).astype(BF)
            parts.append(nn(hot, terms))
        mains = [part[:, :128].reshape(NY, 2, RG, 128) for part in parts]
        tail = jnp.concatenate([part[:, 128:] for part in parts], axis=1).reshape(NY, 2, RG, 128)
        for h in range(2):
            part_s[h, :, i * PR:(i + 1) * PR, :] = jnp.concatenate(
                [mains[0][:, h], mains[1][:, h], tail[:, h]], axis=1).astype(BF)
        if i < YF:
            loop(1, NY, lambda k: z_copy(i, lax.rem(y + k, NY), y).start())
            part_z[y, :, i * PR:(i + 1) * PR, :] = part_s[:, y, i * PR:(i + 1) * PR, :]
        else:
            px_copy(i).start()

    loop(1, NC, lambda k: c2_copy(chip, lax.rem(chip + NC - k, NC)).wait_recv())

    dn_row16[...] = dn_row[...].reshape(32, 128).astype(BF)

    def g2_copy(t, s):
        return grp_copy(dn_row16, dn_g2.at[s], g2_ss.at[t], g2_rs.at[s], t)

    loop(1, NG, lambda k: g2_copy(lax.rem(g + k, NG), g).start())
    dn_g2[g] = dn_row16[...]

    for i in range(YF, FP):
        rows = slice(i * PR, (i + 1) * PR)
        px_copy(i).wait_recv()
        part_y[:, rows, :] = (part_s[xh, :, rows, :].astype(F32) + part_x[:, rows, :].astype(F32)).astype(BF)
        loop(1, NY, lambda k: p_copy(i, lax.rem(y + k, NY), y).start())
    loop(NC, NE, n_send)
    part_r[y, YF * PR:, :] = part_y[y, YF * PR:, :]

    for i in range(YF):
        rows = slice(i * PR, (i + 1) * PR)
        loop(1, NY, lambda k: z_copy(i, y, lax.rem(y + NY - k, NY)).wait_recv())
        total = part_z[0, :, rows, :].astype(F32)
        for s in range(1, NY):
            total = total + part_z[s, :, rows, :].astype(F32)
        part_t[:, rows, :] = total
        part_w[rows, :] = part_t[1 - xh, rows, :].astype(BF)
        w_copy(i).start()

    loop(1, NG, lambda k: g2_copy(g, lax.rem(g + NG - k, NG)).wait_recv())

    def half(h, value):
        dn_full[pl.ds(pl.multiple_of(h * HALF, HALF), HALF), :] = value

    half(core, dn_g2[...].astype(F32).reshape(HALF, 128))
    pair2 = emb_copy(
        dn_full.at[pl.ds(mine, HALF)], dn_full.at[pl.ds(mine, HALF)], pl_ss, pl_rs, mate, e)
    pair2.start()

    for i in range(FP):
        rows = slice(i * PR, (i + 1) * PR)
        if i < YF:
            w_copy(i).wait_recv()
            total = part_t[xh, rows, :] + part_v[rows, :].astype(F32)
        else:
            loop(1, NY, lambda k: p_copy(i, y, lax.rem(y + NY - k, NY)).wait_recv())
            total = part_r[0, rows, :].astype(F32)
            for s in range(1, NY):
                total = total + part_r[s, rows, :].astype(F32)
        tail = total[2 * RG:]
        out_table[2 * i] = jnp.concatenate([total[:RG], tail[:, :64]], axis=1)
        out_table[2 * i + 1] = jnp.concatenate([total[RG:2 * RG], tail[:, 64:]], axis=1)

    loop(1, NE, lambda k: n_copy(e, lax.rem(e + NE - k, NE)).wait_recv())

    pair2.wait_recv()

    pair1.wait_send()
    pair2.wait_send()

    def drain_emb(k):
        t = lax.rem(e + k, NE)
        ids_copy(t, e).wait_send()
        n_copy(t, e).wait_send()
        for q in range(QUADS):
            d_copy(q, t, e).wait_send()

    def drain_chip(k):
        t = lax.rem(chip + k, NC)
        c1_copy(t, chip).wait_send()
        c2_copy(t, chip).wait_send()

    def drain_grp(k):
        t = lax.rem(g + k, NG)
        g1_copy(t, g).wait_send()
        g2_copy(t, g).wait_send()

    loop(1, NE, drain_emb)
    loop(1, NC, drain_chip)
    loop(1, NG, drain_grp)
    for i in range(FP):
        if i < YF:
            loop(1, NY, lambda k: z_copy(i, lax.rem(y + k, NY), y).wait_send())
            w_copy(i).wait_send()
        else:
            px_copy(i).wait_send()
            loop(1, NY, lambda k: p_copy(i, lax.rem(y + k, NY), y).wait_send())


def finish(recv_n, table, dense, out_next, out_table, out_fm, out_proj, out_lcb, out_gain):
    @pl.when(pl.program_id(0) == 0)
    def _():
        out_table[...] = table[...]
        factor = 1.0 / (B * NE * NG)
        for h in range(2):
            rows = pl.ds(128 * h, 128)
            out_fm[rows, :] = jnp.transpose(dense[128 * h:128 * h + 128, :] * factor)
            for w in range(2):
                out_lcb[rows, 128 * w:128 * w + 128] = jnp.transpose(
                    dense[256 + 256 * h + 128 * w:384 + 256 * h + 128 * w, :] * factor)
        out_proj[...] = dense[768:960, :] * factor
        out_gain[...] = jnp.concatenate([dense[960:961, :], dense[968:969, :64]], axis=1) * factor

    tail = recv_n[:, 32:48, :].astype(F32)
    for i in range(2):
        main = recv_n[:, 16 * i:16 * i + 16, :].astype(F32)
        tails = jnp.transpose(tail[:, 8 * i:8 * i + 8].reshape(NF, 128)).astype(BF)
        for p in range(2):
            out_next[p, i, 0:128, :] = jnp.transpose(main[:, 8 * p:8 * p + 8].reshape(NF, 128)).astype(BF)
            out_next[p, i, 128:192, :] = tails[64 * p:64 * p + 64]


def whole(*shape):
    return pl.BlockSpec(shape, lambda q: (0,) * len(shape))


def local(pooled, upstream, ids_now, ids_next, tables, w_fm, w_proj, w_lcb, gain):
    vmem = pl.BlockSpec(memory_space=pltpu.VMEM)
    anywhere = pl.BlockSpec(memory_space=pltpu.HBM)
    dma = pltpu.SemaphoreType.DMA
    scratch = [
        pltpu.VMEM((B, D, NF), BF), pltpu.VMEM((B, D, NF), BF), pltpu.VMEM((FL, D, ROWS), BF),
        pltpu.VMEM((NF, K), BF), pltpu.VMEM((D, K), BF), pltpu.VMEM((NF, NF), BF), pltpu.VMEM((1, D), F32),
        pltpu.VMEM((B, NF), jnp.int32), pltpu.VMEM((B, NF), jnp.int32), pltpu.VMEM((128, NF), jnp.int32),
        pltpu.VMEM((NE, 8, 128), jnp.int32),
        pltpu.VMEM((NE, 8, 128), jnp.int32), pltpu.VMEM((8, KK), jnp.int32),
        pltpu.VMEM((128, 128), jnp.int32),
        pltpu.VMEM((NE * 128, 128), F32), pltpu.VMEM((NE * 64, 128), F32),
        pltpu.VMEM((NE, CH, 128), BF),
        pltpu.VMEM((NE, CH, 128), BF), pltpu.VMEM((NE, CH, 128), BF),
        pltpu.VMEM((2, NY, FP * PR, 128), BF), pltpu.VMEM((NY, FP * PR, 128), BF),
        pltpu.VMEM((NY, FP * PR, 128), BF), pltpu.VMEM((NY, FP * PR, 128), BF),
        pltpu.VMEM((NY, 2, YF * PR, 128), BF), pltpu.VMEM((2, YF * PR, 128), F32),
        pltpu.VMEM((YF * PR, 128), BF), pltpu.VMEM((YF * PR, 128), BF),
        pltpu.VMEM((K, NF), F32), pltpu.VMEM((D, K), F32), pltpu.VMEM((NF, NF), F32), pltpu.VMEM((D, 128), F32),
        pltpu.VMEM((K, NF), BF), pltpu.VMEM((K, D), BF), pltpu.VMEM((D, 128), F32),
        pltpu.VMEM((2 * HALF, 128), F32), pltpu.VMEM((HALF, 128), F32), pltpu.VMEM((NG, 32, 128), F32),
        pltpu.VMEM((NC, 2, 128), F32), pltpu.VMEM((2, 128), F32), pltpu.VMEM((NC, 2, 128), F32),
        pltpu.VMEM((NC, 2, 128), F32), pltpu.VMEM((32, 128), BF), pltpu.VMEM((NG, 32, 128), BF),
        dma((9,)), dma((NE,)), dma((NE,)), dma((NE,)), dma((NE,)), dma((QUADS, NE)), dma((QUADS, NE)),
        dma((FP,)), dma((FP,)), dma((FP, NY)), dma((FP, NY)),
        dma((YF, NY)), dma((YF, NY)), dma((YF,)), dma((YF,)), dma, dma, dma((NG,)), dma((NG,)), dma((NC,)), dma((NC,)),
        dma((NC,)), dma((NC,)), dma((NG,)), dma((NG,)), dma, dma,
    ]
    held = pl.pallas_call(
        kernel,
        out_shape=(
            jax.ShapeDtypeStruct((NE, CH, 128), BF),
            jax.ShapeDtypeStruct((FL, RG, D), F32),
            jax.ShapeDtypeStruct((2 * HALF, 128), F32),
        ),
        in_specs=[anywhere] * 9,
        out_specs=[vmem] * 3,
        scratch_shapes=scratch,
        compiler_params=pltpu.CompilerParams(
            collective_id=0, has_side_effects=True, vmem_limit_bytes=62 << 20),
        name="layer_and_tables",
    )(
        jnp.swapaxes(pooled, 1, 2), jnp.swapaxes(upstream, 1, 2), ids_now, ids_next,
        jnp.swapaxes(tables, 1, 2), w_fm, w_proj.T, w_lcb, gain.reshape(1, D))
    outs = pl.pallas_call(
        finish,
        out_shape=(
            jax.ShapeDtypeStruct((2, J, D, NF), BF),
            jax.ShapeDtypeStruct((FL, RG, D), F32),
            jax.ShapeDtypeStruct((NF, K), F32),
            jax.ShapeDtypeStruct((D, K), F32),
            jax.ShapeDtypeStruct((NF, NF), F32),
            jax.ShapeDtypeStruct((1, D), F32),
        ),
        grid=(QUADS,),
        in_specs=[pl.BlockSpec((NE, QR, 128), lambda q: (0, q, 0)), whole(FL, RG, D), whole(2 * HALF, 128)],
        out_specs=[
            pl.BlockSpec((2, 2, D, NF), lambda q: (0, q, 0, 0)), whole(FL, RG, D), whole(NF, K), whole(D, K),
            whole(NF, NF), whole(1, D)],
        compiler_params=pltpu.CompilerParams(vmem_limit_bytes=62 << 20),
        name="finish",
    )(*held)
    return (
        jnp.swapaxes(outs[0].reshape(B, D, NF), 1, 2), outs[1], outs[2], outs[3].T, outs[4], outs[5].reshape(D))


def solution(mesh):
    return jax.shard_map(
        local,
        mesh=mesh,
        in_specs=(
            P(("grp", "emb"), None, None),
            P(("grp", "emb"), None, None),
            P(("grp", "emb"), None),
            P(("grp", "emb"), None),
            P("emb", None, None),
            P(),
            P(),
            P(),
            P(),
        ),
        out_specs=(P(("grp", "emb"), None, None), P("emb", "grp", None), P(), P(), P(), P()),
        check_vma=False,
    )
```
